256 devices in a mesh: grp: 4 (over y), dev: 64 (over x, z, core).
Axes of the slice: x: 4, y: 4, z: 8, core: 2. Of those that a mesh axis runs over, the one named last changes fastest.
Arguments:
- enc_states: bfloat16 [128, 96, 2048], P('dev'), may hold values from -6 to 6
- norm_gain: float32 [2048], replicated, may hold values from 0.4 to 1.6
- final_gain: float32 [2048], replicated, may hold values from 0.4 to 1.6
- expert_ids: int32 [128, 96, 2], P('dev'), may hold values from 0 to 63, all different within a row; in each aligned block of 192 rows (0 to 191, 192 to 383, ..., all dimensions but the last counted through in order) at most 8 rows name the same one
- expert_gates: float32 [128, 96, 2], P('dev'), may hold values from 0.2 to 1
- source_lengths: int32 [128], P('dev'), may hold values from 12 to 96, as said below
- w_in: bfloat16 [64, 2048, 4096], P('dev', None, 'grp'), may hold values from -0.125 to 0.125
- w_out: bfloat16 [64, 4096, 2048], P('dev', 'grp'), may hold values from -0.09375 to 0.09375
- w_key: bfloat16 [2048, 2048], P('dev', 'grp'), may hold values from -0.125 to 0.125
- w_value: bfloat16 [2048, 2048], P('dev', 'grp'), may hold values from -0.125 to 0.125
- cross_query: bfloat16 [128, 2048], P('dev', 'grp'), may hold values from -6 to 6
Outputs:
- encoded: bfloat16 [128, 96, 2048], P('dev')
- context: bfloat16 [128, 2048], P('dev', 'grp')
The draws below stay inside these ranges and needn't reach their ends.
Inputs may be any that keep to these rules, and one draw needn't show every extreme that they name: `expert_ids`: among the 384 choices of the positions of one index of dev (padded positions included), no expert is named more than 8 times, a bound that some block reaches. `source_lengths`: some sentence has exactly 96 tokens.
All inputs are finite; a program needn't handle non-finite values.
Results may differ from the reference program's by a relative error of at most 0.017.
Values may be sent and summed in bfloat16 or wider, within the bound.
A program may use at most 64 MiB of HBM per device.

```python
import math
import jax
import jax.numpy as jnp
import numpy as np
from jax import lax

D = 2048
HEADS = 16
HEAD_DIM = 128
FF = 4096
EXPERTS = 64
SENT_DEV = 2
LEN = 96
SENT = 128
CAP = 8
N_DEV = 64


def draw_source_lengths(key, part):
    key = jax.random.fold_in(key, 5)
    first_key, second_key = jax.random.split(key)
    lengths = jax.random.randint(first_key, (SENT,), LEN // 8, LEN + 1)
    where_full = jax.random.randint(second_key, (), 0, SENT)
    return lengths.at[where_full].set(LEN).astype(jnp.int32)


def steps_of(key, shape, shards, least, largest):
    gain = 1.0
    for dim, parts in shards:
        heights = jax.random.uniform(jax.random.fold_in(jax.random.fold_in(key, 6), dim), (parts,), jnp.float32, least / len(shards), largest / len(shards))
        gain = gain * jnp.repeat(jnp.exp(heights), shape[dim] // parts).reshape((-1,) + (1,) * (len(shape) - 1 - dim))
    return gain


def deal_out(rng, own, number, rows, amount, top, most, slope):
    sequence = jax.random.permutation(rng, amount)
    packed, ordinary = load_shares(amount, rows * top, most, slope, True), load_shares(amount, rows * top, most, slope, False)
    places = jnp.arange(amount)

    def named(sizes, rotation):
        used = int((sizes > 0).sum())
        fixed = max(1, used // 4)
        passed = fixed + (places - fixed + rotation * (used - fixed)) % max(1, amount - fixed)
        return jnp.zeros((amount,), jnp.int32).at[sequence[jnp.where(places < fixed, places, passed)]].set(jnp.asarray(sizes, jnp.int32))

    sizes = jnp.where(number % 4 == 0, named(packed, number // 4), named(ordinary, number - number // 4 - 1))
    mixed = jax.random.permutation(jax.random.fold_in(own, 3), amount)
    donor, receiver = mixed[0:amount // 2 * 2:2], mixed[1:amount // 2 * 2:2]
    room = jnp.minimum(sizes[donor] - 1, most - sizes[receiver]) // 2
    room = jnp.where((donor == sequence[0]) | (receiver == sequence[0]) | (sizes[receiver] == 0), 0, jnp.maximum(room, 0))
    passed = jax.random.randint(jax.random.fold_in(own, 4), (amount // 2,), 0, 1 << 20) % (room + 1)
    sizes = sizes.at[donor].add(-passed).at[receiver].add(passed)
    items = jnp.searchsorted(jnp.cumsum(sizes), jnp.arange(rows * top), side="right").astype(jnp.int32)
    table = items.reshape(top, rows).T
    table = table[jax.random.permutation(jax.random.fold_in(own, 1), rows)]
    rotation = jax.random.randint(jax.random.fold_in(own, 2), (rows, 1), 0, top)
    return jnp.take_along_axis(table, (jnp.arange(top)[None, :] + rotation) % top, axis=1)


def load_shares(amount, total, limit, slope, full):
    portions = [(1 << 20) // math.isqrt(grade ** slope) + 1 for grade in range(1, amount + 1)]
    largest = limit if full else min(limit, max(-(-total // amount), total * portions[0] // sum(portions)))
    least = 1 if total - largest >= amount - 1 else 0
    holding, spare = [largest] + [least] * (amount - 1), total - largest - least * (amount - 1)
    while spare > 0:
        movable = [i for i in range(1, amount) if holding[i] < largest] or [i for i in range(1, amount) if holding[i] < limit]
        mass, remaining = sum([portions[i] for i in movable]), spare
        for i in movable:
            addition = min(limit - holding[i], max(1, remaining * portions[i] // mass), spare)
            holding[i] = holding[i] + addition
            spare = spare - addition
    return np.array(holding)


def centred(rng, dims, width, bound, shards=(), kind=jnp.bfloat16):
    gain = steps_of(rng, dims, shards, -0.22, 0.18) if shards else 1.0
    values = jax.random.normal(rng, dims, jnp.float32) * width * gain
    return jnp.minimum(jnp.maximum(values, -bound), bound).astype(kind)


def setup_inputs(seed: int = 0) -> dict:
    splits = jax.random.split(jax.random.key(seed), 12)
    enc_states = centred(splits[0], (SENT, LEN, D), 1.0, 6.0, ((0, 64),))
    norm_gain = jnp.clip(1.0 + 0.12 * jax.random.normal(splits[1], (D,), jnp.float32), 0.4, 1.6)
    final_gain = jnp.clip(1.0 + 0.12 * jax.random.normal(splits[2], (D,), jnp.float32), 0.4, 1.6)
    expert_ids_keys = jax.random.split(jax.random.fold_in(splits[3], 1), SENT * LEN // (SENT_DEV * LEN))
    expert_ids_turns = jax.random.permutation(jax.random.fold_in(splits[3], 3), SENT * LEN // (SENT_DEV * LEN))
    expert_ids = jax.vmap(lambda own, number: deal_out(jax.random.fold_in(splits[3], 2), own, number, SENT_DEV * LEN, EXPERTS, 2, CAP, 2))(expert_ids_keys, expert_ids_turns).reshape((SENT, LEN, 2))
    expert_gates = jnp.clip(0.2 + 0.8 * jax.random.uniform(splits[4], (SENT, LEN, 2), jnp.float32) ** steps_of(splits[4], (SENT, LEN, 2), ((0, 64),), -0.2, 0.2), 0.2, 1.0)
    source_lengths = draw_source_lengths(jax.random.fold_in(splits[11], 71), 0)
    w_in = centred(splits[6], (EXPERTS, D, FF), D ** -0.5, 0.125, ((0, 64), (2, 4)))
    w_out = centred(splits[7], (EXPERTS, FF, D), FF ** -0.5, 0.09375, ((0, 64), (1, 4)))
    w_key = centred(splits[8], (D, D), D ** -0.5, 0.125, ((0, 64), (1, 4)))
    w_value = centred(splits[9], (D, D), D ** -0.5, 0.125, ((0, 64), (1, 4)))
    cross_query = centred(splits[10], (SENT, D), 1.0, 6.0, ((0, 64), (1, 4)))
    return dict(enc_states=enc_states, norm_gain=norm_gain, final_gain=final_gain, expert_ids=expert_ids, expert_gates=expert_gates, source_lengths=source_lengths, w_in=w_in, w_out=w_out, w_key=w_key, w_value=w_value, cross_query=cross_query)


norm_epsilon = 1e-05

def layer_norm(values, gain_vector):
    average = lax.optimization_barrier(jnp.mean(values, axis=-1, keepdims=True))
    centered = values - average
    variance = lax.optimization_barrier(jnp.mean(centered * centered, axis=-1, keepdims=True))
    return centered * lax.rsqrt(variance + norm_epsilon) * gain_vector

def reference(enc_states, norm_gain, final_gain, expert_ids, expert_gates, source_lengths, w_in, w_out, w_key, w_value, cross_query):
    token_count = SENT * LEN
    states = enc_states.reshape(token_count, D).astype(jnp.float32)
    normed = layer_norm(states, norm_gain).astype(jnp.bfloat16)
    positions = jnp.arange(LEN, dtype=jnp.int32)
    live_mask = positions[None, :] < source_lengths[:, None]
    chosen = expert_ids.reshape(token_count * 2).astype(jnp.int32)
    gate_flat = (expert_gates * live_mask[:, :, None].astype(jnp.float32)).reshape(token_count * 2)
    ordering = jnp.argsort(chosen, stable=True).astype(jnp.int32)
    counts = lax.optimization_barrier(jnp.sum((chosen[:, None] == jnp.arange(EXPERTS, dtype=jnp.int32)[None, :]).astype(jnp.int32), axis=0))
    starts = (jnp.cumsum(counts) - counts).astype(jnp.int32)
    most_rows = N_DEV * CAP
    assigned = token_count * 2

    def add_expert(mixture, inputs):
        weight_in, weight_out, expert_index = inputs
        slot_range = jnp.arange(most_rows, dtype=jnp.int32)
        in_range = slot_range < counts[expert_index]
        picked = ordering[jnp.minimum(starts[expert_index] + slot_range, assigned - 1)]
        token_rows = (picked // 2).astype(jnp.int32)
        hidden = jnp.maximum(jnp.dot(normed[token_rows], weight_in, preferred_element_type=jnp.float32), 0.0).astype(jnp.bfloat16)
        outputs = jnp.dot(hidden, weight_out, preferred_element_type=jnp.float32)
        outputs = outputs * jnp.where(in_range, gate_flat[picked], jnp.zeros_like(gate_flat[picked]))[:, None]
        return (mixture.at[token_rows].add(outputs), None)
    mixture, unused = lax.scan(add_expert, jnp.zeros((token_count, D), jnp.float32), (w_in, w_out, jnp.arange(EXPERTS, dtype=jnp.int32)))
    encoded = layer_norm(states + mixture, final_gain).astype(jnp.bfloat16)
    key_cache = jnp.dot(encoded, w_key, preferred_element_type=jnp.float32).astype(jnp.bfloat16).reshape(SENT, LEN, HEADS, HEAD_DIM)
    value_cache = jnp.dot(encoded, w_value, preferred_element_type=jnp.float32).astype(jnp.bfloat16).reshape(SENT, LEN, HEADS, HEAD_DIM)
    queries = cross_query.reshape(SENT, HEADS, HEAD_DIM).astype(jnp.float32)
    scores = jnp.einsum('shd,sthd->sht', queries, key_cache.astype(jnp.float32)) * (1.0 / math.sqrt(HEAD_DIM))
    weights = jnp.exp(scores) * live_mask[:, None, :].astype(jnp.float32)
    probabilities = (weights / lax.optimization_barrier(jnp.sum(weights, axis=-1, keepdims=True))).astype(jnp.bfloat16)
    context = jnp.einsum('sht,sthd->shd', probabilities.astype(jnp.float32), value_cache.astype(jnp.float32))
    return (encoded.reshape(SENT, LEN, D), context.astype(jnp.bfloat16).reshape(SENT, D))
```

```python
import functools
import math

import jax
import jax.numpy as jnp
from jax import lax
from jax.experimental import pallas as pl
from jax.experimental.pallas import tpu as pltpu
from jax.sharding import PartitionSpec as P

HEADS = 16
CAPACITY = 8
EPSILON = 1e-05
F32 = jnp.float32
BF16 = jnp.bfloat16
MESH = pl.DeviceIdType.MESH


def moe_kernel(
    n_exp,
    n_x,
    enc_ref,
    ngain_ref,
    fgain_ref,
    ids_ref,
    gates_ref,
    lens_ref,
    win_hbm,
    wout_hbm,
    out_ref,
    win,
    wout,
    normed,
    dispatch,
    xbuf,
    combine,
    xrow,
    hid,
    part,
    st1,
    rv1,
    st2,
    rv2,
    back,
    ybuf,
    mix,
    w_sem,
    a2a_send,
    a2a_recv,
    yag_send,
    yag_recv,
    rs_send,
    rs_recv,
    ret_send,
    ret_recv,
    mix_send,
    mix_recv,
):
    rows, width = enc_ref.shape
    sent = lens_ref.shape[0]
    length = rows // sent
    quarter = width // 4
    half = quarter // 2
    per = n_exp // n_x
    crow = per * CAPACITY
    mrow = per * 2 * CAPACITY
    prow = normed.shape[0]

    g = lax.axis_index("grp")
    d = lax.axis_index("dev")
    my_x = d // per
    my_z = d % per
    right, left, diag = (g + 1) % 4, (g + 3) % 4, (g + 2) % 4

    load_in = pltpu.make_async_copy(win_hbm, win, w_sem.at[0])
    load_out = pltpu.make_async_copy(wout_hbm, wout, w_sem.at[1])
    load_in.start()
    load_out.start()

    barrier = pltpu.get_barrier_semaphore()

    def greet(i, carry):
        pl.semaphore_signal(barrier, inc=1, device_id=(g, (d + i) % n_exp), device_id_type=MESH)
        return carry

    lax.fori_loop(1, n_exp, greet, 0)
    for i in range(1, 4):
        pl.semaphore_signal(barrier, inc=1, device_id=((g + i) % 4, d), device_id_type=MESH)

    blk = 16
    qcols = pl.ds(pl.multiple_of(g * quarter, 128), quarter)

    def norm_block(i, carry):
        r = pl.ds(pl.multiple_of(i * blk, blk), blk)
        v = enc_ref[r, :].astype(F32)
        mean = jnp.mean(v, axis=-1, keepdims=True)
        c = v - mean
        var = jnp.mean(c * c, axis=-1, keepdims=True)
        own = enc_ref[r, qcols].astype(F32) - mean
        own = own * lax.rsqrt(var + EPSILON) * ngain_ref[:, qcols]
        normed[r, :] = own.astype(BF16)
        return carry

    lax.fori_loop(0, rows // blk, norm_block, 0)
    if prow > rows:
        normed[rows:, :] = jnp.zeros((prow - rows, quarter), BF16)

    pos = lax.broadcasted_iota(jnp.int32, (rows, 1), 0)
    live = jnp.zeros((rows, 1), jnp.bool_)
    for s in range(sent):
        live = live | ((pos >= s * length) & (pos < s * length + lens_ref[s]))
    lane = lax.broadcasted_iota(jnp.int32, (rows, 128), 1)
    earlier = (
        lax.broadcasted_iota(jnp.int32, (rows, rows), 0)
        > lax.broadcasted_iota(jnp.int32, (rows, rows), 1)
    ).astype(BF16)
    codes = []
    offset = jnp.zeros((1, 128), F32)
    for k in range(2):
        hot = jnp.where((ids_ref[:, k : k + 1] == lane) & live, 1.0, 0.0).astype(F32)
        rank = jnp.dot(earlier, hot.astype(BF16), preferred_element_type=F32) + offset
        offset = offset + jnp.sum(hot, axis=0, keepdims=True)
        code = jnp.sum(
            hot * (rank + (2 * CAPACITY) * lane.astype(F32)), axis=1, keepdims=True
        )
        codes.append(jnp.where(live, code, -100.0))
    cols = jnp.where(lane == 0, codes[0], jnp.where(lane == 1, codes[1], -100.0))
    if prow > rows:
        cols = jnp.concatenate([cols, jnp.full((prow - rows, 128), -100.0, F32)], axis=0)
    trow = cols.T.astype(jnp.int32)
    row0, row1 = trow[0:1, :], trow[1:2, :]
    code0, code1 = codes[0].astype(jnp.int32), codes[1].astype(jnp.int32)
    gate0, gate1 = gates_ref[:, 0:1], gates_ref[:, 1:2]

    pl.semaphore_wait(barrier, n_exp - 1 + 3)

    for c in range(n_x):
        base = ((my_x + c) % n_x) * mrow
        r = lax.broadcasted_iota(jnp.int32, (mrow, prow), 0) + base
        acc = jnp.zeros((mrow, half), F32)
        for h in range(2):
            rh = r - h * CAPACITY
            pick = jnp.where((rh == row0) | (rh == row1), 1.0, 0.0).astype(BF16)
            acc = acc + jnp.dot(
                pick, normed[:, h * half : (h + 1) * half], preferred_element_type=F32
            )
        dispatch[c] = acc.astype(BF16).reshape(per, 2 * CAPACITY, half)

        def send(j, carry, c=c):
            z = (my_z + j) % per
            pltpu.make_async_remote_copy(
                src_ref=dispatch.at[c, z],
                dst_ref=xbuf.at[g, d],
                send_sem=a2a_send.at[c],
                recv_sem=a2a_recv.at[c],
                device_id=(g, ((my_x + c) % n_x) * per + z),
                device_id_type=MESH,
            ).start()
            return carry

        if c == 0:
            pltpu.make_async_copy(
                dispatch.at[0, my_z], xbuf.at[g, d], a2a_recv.at[0]
            ).start()
            lax.fori_loop(1, per, send, 0)
        else:
            lax.fori_loop(0, per, send, 0)

    for c in range(n_x):
        base = ((my_x + c) % n_x) * mrow
        col = lax.broadcasted_iota(jnp.int32, (rows, mrow), 1) + base
        for h in range(2):
            ch = col - h * CAPACITY
            value = jnp.where(ch == code0, gate0, jnp.where(ch == code1, gate1, 0.0))
            high = value.astype(BF16)
            combine[c, 2 * h * rows : (2 * h + 1) * rows, :] = high
            combine[c, (2 * h + 1) * rows : (2 * h + 2) * rows, :] = (
                value - high.astype(F32)
            ).astype(BF16)

    def slab(c):
        return ((my_x + n_x - c) % n_x) * per

    def ycopy(src, dst, send_sem, recv_sem, to):
        return pltpu.make_async_remote_copy(
            src_ref=src,
            dst_ref=dst,
            send_sem=send_sem,
            recv_sem=recv_sem,
            device_id=(to, d),
            device_id_type=MESH,
        )

    def xs(q, c, start=0, size=per):
        return xbuf.at[q, pl.ds(slab(c) + start, size)]

    def arrived(ref, sem):
        pltpu.make_async_copy(ref, ref, sem).wait()

    hp = per // 2
    sends = []

    def stage_a(c):
        arrived(xs(g, c), a2a_recv.at[c])
        for i, to in enumerate((right, left)):
            cp = ycopy(xs(g, c), xs(g, c), yag_send.at[c, i], yag_recv.at[c, i], to)
            cp.start()
            sends.append(cp)

    def stage_b(c):
        arrived(xs(left, c), yag_recv.at[c, 0])
        cp = ycopy(
            xs(left, c, 0, hp), xs(left, c, 0, hp), yag_send.at[c, 2], yag_recv.at[c, 2], right
        )
        cp.start()
        sends.append(cp)
        arrived(xs(right, c), yag_recv.at[c, 1])
        cp = ycopy(
            xs(right, c, hp, hp), xs(right, c, hp, hp), yag_send.at[c, 3], yag_recv.at[c, 3], left
        )
        cp.start()
        sends.append(cp)

    hrow = crow // 2

    def stage_c(c):
        arrived(xs(diag, c, 0, hp), yag_recv.at[c, 2])
        arrived(xs(diag, c, hp, hp), yag_recv.at[c, 3])
        for q in range(4):
            block = xbuf[q, pl.ds(slab(c), per)].astype(F32)
            for h in range(2):
                xrow[:, q * quarter + h * half : q * quarter + (h + 1) * half] = (
                    block[:, h * CAPACITY : (h + 1) * CAPACITY, :]
                    .reshape(crow, half)
                    .astype(BF16)
                )
        if c == 0:
            load_in.wait()
        tile = min(256, hid.shape[1])

        def first(n, carry):
            cs = pl.ds(pl.multiple_of(n * tile, tile), tile)
            hid[:, cs] = jnp.maximum(
                jnp.dot(xrow[...], win[:, cs], preferred_element_type=F32), 0.0
            ).astype(BF16)
            return carry

        lax.fori_loop(0, hid.shape[1] // tile, first, 0)
        if c == 0:
            load_out.wait()

        def second(q):
            cs = pl.ds(pl.multiple_of(q * quarter, 128), quarter)
            return jnp.dot(hid[...], wout[:, cs], preferred_element_type=F32)

        st1[c] = second(diag).astype(BF16)
        for i, to in enumerate((right, left)):
            cp = ycopy(
                st1.at[c, pl.ds(i * hrow, hrow)],
                rv1.at[c, pl.ds(i * hrow, hrow)],
                rs_send.at[c, i],
                rs_recv.at[c, i],
                to,
            )
            cp.start()
            sends.append(cp)

        part[c, 0] = second(right)
        part[c, 1] = second(left)
        part[c, 2] = second(g)

    def stage_d(c):
        for i, to in enumerate((right, left)):
            a, b = i * hrow, (1 - i) * hrow
            arrived(rv1.at[c, pl.ds(a, hrow)], rs_recv.at[c, i])
            st2[c, i, a : a + hrow, :] = (
                part[c, i, a : a + hrow, :] + rv1[c, a : a + hrow, :].astype(F32)
            ).astype(BF16)
            st2[c, i, b : b + hrow, :] = part[c, i, b : b + hrow, :].astype(BF16)
            cp = ycopy(st2.at[c, i], rv2.at[c, i], rs_send.at[c, 2 + i], rs_recv.at[c, 2 + i], to)
            cp.start()
            sends.append(cp)

    def stage_e(c):
        for i in range(2):
            arrived(rv2.at[c, i], rs_recv.at[c, 2 + i])
        total = part[c, 2] + rv2[c, 0].astype(F32) + rv2[c, 1].astype(F32)
        total = total.reshape(per, CAPACITY, quarter)
        back[c] = jnp.concatenate([total[:, :, :half], total[:, :, half:]], axis=1).astype(BF16)

        def send(j, carry):
            z = (my_z + j) % per
            pltpu.make_async_remote_copy(
                src_ref=back.at[c, z],
                dst_ref=ybuf.at[d],
                send_sem=ret_send.at[c],
                recv_sem=ret_recv.at[c],
                device_id=(g, slab(c) + z),
                device_id_type=MESH,
            ).start()
            return carry

        if c == 0:
            pltpu.make_async_copy(back.at[0, my_z], ybuf.at[d], ret_recv.at[0]).start()
            lax.fori_loop(1, per, send, 0)
        else:
            lax.fori_loop(0, per, send, 0)

    stages = (stage_a, stage_b, stage_c, stage_d, stage_e)
    for step in range(n_x + len(stages) - 1):
        for k in reversed(range(len(stages))):
            if 0 <= step - k < n_x:
                stages[k](step - k)

    acc = jnp.zeros((4 * rows, half), F32)
    for c in range(n_x):
        here = pl.ds(((my_x + c) % n_x) * per, per)
        arrived(ybuf.at[here], ret_recv.at[c])
        acc = acc + jnp.dot(
            combine[c], ybuf[here].reshape(mrow, half), preferred_element_type=F32
        )
    mix[g] = jnp.concatenate(
        [acc[:rows] + acc[rows : 2 * rows], acc[2 * rows : 3 * rows] + acc[3 * rows :]], axis=1
    ).astype(BF16)

    hm = rows // 2
    for i, to in enumerate((right, left)):
        cp = ycopy(mix.at[g], mix.at[g], mix_send.at[i], mix_recv.at[i], to)
        cp.start()
        sends.append(cp)
    for i, (origin, to) in enumerate(((left, right), (right, left))):
        arrived(mix.at[origin], mix_recv.at[i])
        piece = mix.at[origin, pl.ds(i * hm, hm)]
        cp = ycopy(piece, piece, mix_send.at[2 + i], mix_recv.at[2 + i], to)
        cp.start()
        sends.append(cp)
    for i in range(2):
        arrived(mix.at[diag, pl.ds(i * hm, hm)], mix_recv.at[2 + i])

    def final_block(i, carry):
        r = pl.ds(pl.multiple_of(i * blk, blk), blk)
        m = jnp.concatenate([mix[q, r, :] for q in range(4)], axis=1)
        v = enc_ref[r, :].astype(F32) + m.astype(F32)
        mean = jnp.mean(v, axis=-1, keepdims=True)
        cen = v - mean
        var = jnp.mean(cen * cen, axis=-1, keepdims=True)
        out_ref[r, :] = (cen * lax.rsqrt(var + EPSILON) * fgain_ref[...]).astype(BF16)
        return carry

    lax.fori_loop(0, rows // blk, final_block, 0)

    for cp in sends:
        cp.wait_send()
    for c in range(n_x):
        count = per - 1 if c == 0 else per
        for buf, sem in ((dispatch, a2a_send), (back, ret_send)):
            arrived(buf.at[c, pl.ds(0, count)], sem.at[c])


def experts_layer(n_exp, enc, ngain, fgain, ids, gates, lens, w_in, w_out):
    rows, width = enc.shape
    n_x = 4 if n_exp >= 16 else 2
    per = n_exp // n_x
    quarter, half = width // 4, width // 8
    crow, mrow = per * CAPACITY, per * 2 * CAPACITY
    ff = w_in.shape[1]
    prow = -(-rows // 128) * 128
    vmem = pl.BlockSpec(memory_space=pltpu.VMEM)
    hbm = pl.BlockSpec(memory_space=pl.ANY)
    smem = pl.BlockSpec(memory_space=pltpu.SMEM)
    dma = pltpu.SemaphoreType.DMA
    return pl.pallas_call(
        functools.partial(moe_kernel, n_exp, n_x),
        out_shape=jax.ShapeDtypeStruct((rows, width), BF16),
        in_specs=[vmem, vmem, vmem, vmem, vmem, smem, hbm, hbm],
        out_specs=vmem,
        scratch_shapes=[
            pltpu.VMEM(w_in.shape, BF16),
            pltpu.VMEM(w_out.shape, BF16),
            pltpu.VMEM((prow, quarter), BF16),
            pltpu.VMEM((n_x, per, 2 * CAPACITY, half), BF16),
            pltpu.VMEM((4, n_exp, 2 * CAPACITY, half), BF16),
            pltpu.VMEM((n_x, 4 * rows, mrow), BF16),
            pltpu.VMEM((crow, width), BF16),
            pltpu.VMEM((crow, ff), BF16),
            pltpu.VMEM((n_x, 3, crow, quarter), F32),
            pltpu.VMEM((n_x, crow, quarter), BF16),
            pltpu.VMEM((n_x, crow, quarter), BF16),
            pltpu.VMEM((n_x, 2, crow, quarter), BF16),
            pltpu.VMEM((n_x, 2, crow, quarter), BF16),
            pltpu.VMEM((n_x, per, 2 * CAPACITY, half), BF16),
            pltpu.VMEM((n_exp, 2 * CAPACITY, half), BF16),
            pltpu.VMEM((4, rows, quarter), BF16),
            dma((2,)),
            dma((n_x,)),
            dma((n_x,)),
            dma((n_x, 4)),
            dma((n_x, 4)),
            dma((n_x, 4)),
            dma((n_x, 4)),
            dma((n_x,)),
            dma((n_x,)),
            dma((4,)),
            dma((4,)),
        ],
        compiler_params=pltpu.CompilerParams(
            collective_id=0, has_side_effects=True, vmem_limit_bytes=48 * 1024 * 1024
        ),
        cost_estimate=pl.CostEstimate(
            flops=4 * n_exp * CAPACITY * width * ff,
            bytes_accessed=200_000_000,
            transcendentals=0,
        ),
    )(enc, ngain, fgain, ids, gates, lens, w_in, w_out)


def on_device(
    n_exp,
    enc_states,
    norm_gain,
    final_gain,
    expert_ids,
    expert_gates,
    source_lengths,
    w_in,
    w_out,
    w_key,
    w_value,
    cross_query,
):
    sentences, length, model_width = enc_states.shape
    row_count = sentences * length
    key_rows = lax.all_gather(w_key, "dev", axis=0, tiled=True)
    value_rows = lax.all_gather(w_value, "dev", axis=0, tiled=True)
    encoded = experts_layer(
        n_exp,
        enc_states.reshape(row_count, model_width),
        norm_gain.reshape(1, model_width),
        final_gain.reshape(1, model_width),
        expert_ids.reshape(row_count, 2),
        expert_gates.reshape(row_count, 2),
        source_lengths,
        w_in[0],
        w_out[0],
    )
    positions = lax.broadcasted_iota(jnp.int32, (sentences, length), 1)
    live_mask = positions < source_lengths[:, None]
    column_count = w_key.shape[1]
    key_sum = jnp.dot(encoded, key_rows, preferred_element_type=jnp.float32)
    value_sum = jnp.dot(encoded, value_rows, preferred_element_type=jnp.float32)
    head_dim = model_width // HEADS
    local_heads = column_count // head_dim
    key_cache = key_sum.astype(jnp.bfloat16).reshape(sentences, length, local_heads, head_dim)
    value_cache = value_sum.astype(jnp.bfloat16).reshape(sentences, length, local_heads, head_dim)
    queries = cross_query.reshape(sentences, local_heads, head_dim)
    scores = jnp.einsum("shd,sthd->sht", queries, key_cache, preferred_element_type=jnp.float32) * (
        1.0 / math.sqrt(head_dim)
    )
    weights = jnp.exp(scores) * live_mask[:, None, :].astype(jnp.float32)
    probabilities = (weights / jnp.sum(weights, axis=-1, keepdims=True)).astype(jnp.bfloat16)
    context = jnp.einsum(
        "sht,sthd->shd", probabilities, value_cache, preferred_element_type=jnp.float32
    )
    return (
        encoded.reshape(sentences, length, model_width),
        context.astype(jnp.bfloat16).reshape(sentences, column_count),
    )


def solution(mesh):
    return jax.shard_map(
        functools.partial(on_device, mesh.shape["dev"]),
        mesh=mesh,
        in_specs=(
            P("dev", None, None),
            P(),
            P(),
            P("dev", None, None),
            P("dev", None, None),
            P("dev"),
            P("dev", None, "grp"),
            P("dev", "grp", None),
            P("dev", "grp"),
            P("dev", "grp"),
            P("dev", "grp"),
        ),
        out_specs=(P("dev", None, None), P("dev", "grp")),
        check_vma=False,
    )
```

```python
import functools
import math

import jax
import jax.numpy as jnp
from jax import lax
from jax.experimental import pallas as pl
from jax.experimental.pallas import tpu as pltpu
from jax.sharding import PartitionSpec as P

HEADS = 16
HEAD_DIM = 128
CAPACITY = 8
EPSILON = 1e-05
F32 = jnp.float32
BF16 = jnp.bfloat16
MESH = pl.DeviceIdType.MESH


def layer_kernel(
    n_exp,
    n_x,
    lens_ref,
    ids_ref,
    gates_ref,
    query_ref,
    enc_hbm,
    ngain_hbm,
    fgain_hbm,
    wkey_hbm,
    wvalue_hbm,
    win_hbm,
    wout_hbm,
    out_ref,
    context_ref,
    enc_ref,
    ngain_ref,
    fgain_ref,
    wkv,
    win,
    wout,
    qkey,
    normed,
    dispatch,
    xbuf,
    combine,
    xrow,
    hid,
    part,
    st1,
    rv1,
    st2,
    rv2,
    back,
    ybuf,
    mix,
    w_sem,
    a2a_send,
    a2a_recv,
    yag_send,
    yag_recv,
    rs_send,
    rs_recv,
    ret_send,
    ret_recv,
    mix_send,
    mix_recv,
    kvx_send,
    kvx_recv,
    kvz_send,
    kvz_recv,
    kvc_send,
    kvc_recv,
):
    rows, width = enc_ref.shape
    sent, _, length = ids_ref.shape
    quarter = width // 4
    half = quarter // 2
    per = n_exp // n_x
    crow = per * CAPACITY
    mrow = per * 2 * CAPACITY
    prow = normed.shape[0]

    g = lax.axis_index("grp")
    d = lax.axis_index("dev")
    my_x = d // per
    my_z = d % per
    right, left, diag = (g + 1) % 4, (g + 3) % 4, (g + 2) % 4

    loads = [
        pltpu.make_async_copy(src, dst, w_sem.at[i])
        for i, (src, dst) in enumerate(
            (
                (enc_hbm, enc_ref),
                (ngain_hbm, ngain_ref),
                (wkey_hbm, wkv.at[my_x, my_z, 0]),
                (wvalue_hbm, wkv.at[my_x, my_z, 1]),
                (win_hbm, win),
                (wout_hbm, wout),
                (fgain_hbm, fgain_ref),
            )
        )
    ]
    for load in loads:
        load.start()

    barrier = pltpu.get_barrier_semaphore()

    def greet(i, carry):
        pl.semaphore_signal(barrier, inc=1, device_id=(g, (d + i) % n_exp), device_id_type=MESH)
        return carry

    lax.fori_loop(1, n_exp, greet, 0)
    for i in range(1, 4):
        pl.semaphore_signal(barrier, inc=1, device_id=((g + i) % 4, d), device_id_type=MESH)

    def arrived(ref, sem):
        pltpu.make_async_copy(ref, ref, sem).wait()

    loads[0].wait()
    loads[1].wait()

    blk = 16
    qcols = pl.ds(pl.multiple_of(g * quarter, 128), quarter)

    def norm_block(i, carry):
        r = pl.ds(pl.multiple_of(i * blk, blk), blk)
        v = enc_ref[r, :].astype(F32)
        mean = jnp.mean(v, axis=-1, keepdims=True)
        c = v - mean
        var = jnp.mean(c * c, axis=-1, keepdims=True)
        own = enc_ref[r, qcols].astype(F32) - mean
        own = own * lax.rsqrt(var + EPSILON) * ngain_ref[:, qcols]
        normed[r, :] = own.astype(BF16)
        return carry

    lax.fori_loop(0, rows // blk, norm_block, 0)
    if prow > rows:
        normed[rows:, :] = jnp.zeros((prow - rows, quarter), BF16)

    def along(ref, k):
        return jnp.concatenate([ref[i, k : k + 1, :] for i in range(sent)], axis=1)

    pos = lax.broadcasted_iota(jnp.int32, (1, rows), 1)
    live = jnp.zeros((1, rows), jnp.bool_)
    for i in range(sent):
        live = live | ((pos >= i * length) & (pos < i * length + lens_ref[i]))
    expert = lax.broadcasted_iota(jnp.int32, (n_exp, rows), 0)
    earlier = (
        lax.broadcasted_iota(jnp.int32, (rows, rows), 0)
        < lax.broadcasted_iota(jnp.int32, (rows, rows), 1)
    ).astype(BF16)
    codes = []
    offset = jnp.zeros((n_exp, 1), F32)
    for k in range(2):
        hot = jnp.where((along(ids_ref, k) == expert) & live, 1.0, 0.0).astype(F32)
        rank = jnp.dot(hot.astype(BF16), earlier, preferred_element_type=F32) + offset
        offset = offset + jnp.sum(hot, axis=1, keepdims=True)
        code = jnp.sum(
            hot * (rank + (2 * CAPACITY) * expert.astype(F32)), axis=0, keepdims=True
        )
        codes.append(jnp.where(live, code, -100.0))
    line = lax.broadcasted_iota(jnp.int32, (128, rows), 0)
    facts = jnp.zeros((128, rows), F32)
    for i, fact in enumerate(codes + [along(gates_ref, 0), along(gates_ref, 1)]):
        facts = jnp.where(line == i, fact, facts)
    if prow > rows:
        facts = jnp.concatenate([facts, jnp.zeros((128, prow - rows), F32)], axis=1)
        codes = [
            jnp.concatenate([v, jnp.full((1, prow - rows), -100.0, F32)], axis=1) for v in codes
        ]
    row0, row1 = codes[0].astype(jnp.int32), codes[1].astype(jnp.int32)
    columns = facts.T
    code0 = columns[:rows, 0:1].astype(jnp.int32)
    code1 = columns[:rows, 1:2].astype(jnp.int32)
    gate0, gate1 = columns[:rows, 2:3], columns[:rows, 3:4]

    for c in range(n_x):
        base = ((my_x + c) % n_x) * mrow
        r = lax.broadcasted_iota(jnp.int32, (mrow, prow), 0) + base
        acc = jnp.zeros((mrow, half), F32)
        for h in range(2):
            rh = r - h * CAPACITY
            pick = jnp.where((rh == row0) | (rh == row1), 1.0, 0.0).astype(BF16)
            acc = acc + jnp.dot(
                pick, normed[:, h * half : (h + 1) * half], preferred_element_type=F32
            )
        dispatch[c] = acc.astype(BF16).reshape(per, 2 * CAPACITY, half)

    pl.semaphore_wait(barrier, n_exp - 1 + 3)

    for c in range(n_x):

        def send(j, carry, c=c):
            z = (my_z + j) % per
            pltpu.make_async_remote_copy(
                src_ref=dispatch.at[c, z],
                dst_ref=xbuf.at[g, d],
                send_sem=a2a_send.at[c],
                recv_sem=a2a_recv.at[c],
                device_id=(g, ((my_x + c) % n_x) * per + z),
                device_id_type=MESH,
            ).start()
            return carry

        if c == 0:
            pltpu.make_async_copy(
                dispatch.at[0, my_z], xbuf.at[g, d], a2a_recv.at[0]
            ).start()
            lax.fori_loop(1, per, send, 0)
        else:
            lax.fori_loop(0, per, send, 0)

    n_z = per // 2
    my_zz, my_core = my_z // 2, my_z % 2
    kv_sends = []

    def kv_copy(ref, send_sem, recv_sem, to_x, to_z):
        cp = pltpu.make_async_remote_copy(
            src_ref=ref,
            dst_ref=ref,
            send_sem=send_sem,
            recv_sem=recv_sem,
            device_id=(g, to_x * per + to_z),
            device_id_type=MESH,
        )
        cp.start()
        kv_sends.append(cp)

    loads[2].wait()
    loads[3].wait()
    for i in range(1, n_x):
        kv_copy(
            wkv.at[my_x, my_z],
            kvx_send.at[i],
            kvx_recv.at[i],
            (my_x + i) % n_x,
            my_z,
        )

    def kv_piece(way, step, core):
        shift = step if way == 1 else n_z - step
        z = 2 * ((my_zz + shift) % n_z) + core
        if step < n_z // 2 or step == 0:
            return wkv.at[:, z]
        return wkv.at[:, z, way]

    def kv_event(step):
        if step > n_z // 2:
            return
        other = 2 * my_zz + (1 - my_core)
        if step == 0:
            for i in range(1, n_x):
                arrived(wkv.at[(my_x + n_x - i) % n_x, my_z], kvx_recv.at[i])
            kv_copy(kv_piece(0, 0, my_core), kvc_send.at[0, 0], kvc_recv.at[0, 0], my_x, other)
        for way in range(2):
            if step > 0:
                arrived(kv_piece(way, step, my_core), kvz_recv.at[way, step])
            if step < n_z // 2:
                ref = kv_piece(way, step, my_core)
                if step + 1 == n_z // 2:
                    shift = step if way == 1 else n_z - step
                    ref = wkv.at[:, 2 * ((my_zz + shift) % n_z) + my_core, way]
                to = 2 * ((my_zz + (1 if way == 0 else n_z - 1)) % n_z) + my_core
                kv_copy(ref, kvz_send.at[way, step], kvz_recv.at[way, step + 1], my_x, to)
            if step > 0:
                kv_copy(
                    kv_piece(way, step, my_core),
                    kvc_send.at[way, step],
                    kvc_recv.at[way, step],
                    my_x,
                    other,
                )

    def kv_finish():
        arrived(kv_piece(0, 0, 1 - my_core), kvc_recv.at[0, 0])
        for step in range(1, n_z // 2 + 1):
            for way in range(2):
                arrived(kv_piece(way, step, 1 - my_core), kvc_recv.at[way, step])

    for c in range(n_x):
        base = ((my_x + c) % n_x) * mrow
        col = lax.broadcasted_iota(jnp.int32, (rows, mrow), 1) + base
        for h in range(2):
            ch = col - h * CAPACITY
            value = jnp.where(ch == code0, gate0, jnp.where(ch == code1, gate1, 0.0))
            high = value.astype(BF16)
            combine[c, 2 * h * rows : (2 * h + 1) * rows, :] = high
            combine[c, (2 * h + 1) * rows : (2 * h + 2) * rows, :] = (
                value - high.astype(F32)
            ).astype(BF16)

    def slab(c):
        return ((my_x + n_x - c) % n_x) * per

    def ycopy(src, dst, send_sem, recv_sem, to):
        return pltpu.make_async_remote_copy(
            src_ref=src,
            dst_ref=dst,
            send_sem=send_sem,
            recv_sem=recv_sem,
            device_id=(to, d),
            device_id_type=MESH,
        )

    def xs(q, c, start=0, size=per):
        return xbuf.at[q, pl.ds(slab(c) + start, size)]

    hp = per // 2
    sends = []

    def stage_a(c):
        arrived(xs(g, c), a2a_recv.at[c])
        for i, to in enumerate((right, left)):
            cp = ycopy(xs(g, c), xs(g, c), yag_send.at[c, i], yag_recv.at[c, i], to)
            cp.start()
            sends.append(cp)

    def stage_b(c):
        arrived(xs(left, c), yag_recv.at[c, 0])
        cp = ycopy(
            xs(left, c, 0, hp), xs(left, c, 0, hp), yag_send.at[c, 2], yag_recv.at[c, 2], right
        )
        cp.start()
        sends.append(cp)
        arrived(xs(right, c), yag_recv.at[c, 1])
        cp = ycopy(
            xs(right, c, hp, hp), xs(right, c, hp, hp), yag_send.at[c, 3], yag_recv.at[c, 3], left
        )
        cp.start()
        sends.append(cp)

    hrow = crow // 2

    def stage_c(c):
        arrived(xs(diag, c, 0, hp), yag_recv.at[c, 2])
        arrived(xs(diag, c, hp, hp), yag_recv.at[c, 3])
        for q in range(4):
            block = xbuf[q, pl.ds(slab(c), per)].astype(F32)
            for h in range(2):
                xrow[:, q * quarter + h * half : q * quarter + (h + 1) * half] = (
                    block[:, h * CAPACITY : (h + 1) * CAPACITY, :]
                    .reshape(crow, half)
                    .astype(BF16)
                )
        if c == 0:
            loads[4].wait()
        tile = min(256, hid.shape[1])

        def first(n, carry):
            cs = pl.ds(pl.multiple_of(n * tile, tile), tile)
            hid[:, cs] = jnp.maximum(
                jnp.dot(xrow[...], win[:, cs], preferred_element_type=F32), 0.0
            ).astype(BF16)
            return carry

        lax.fori_loop(0, hid.shape[1] // tile, first, 0)
        if c == 0:
            loads[5].wait()

        def second(q):
            cs = pl.ds(pl.multiple_of(q * quarter, 128), quarter)
            return jnp.dot(hid[...], wout[:, cs], preferred_element_type=F32)

        st1[c] = second(diag).astype(BF16)
        for i, to in enumerate((right, left)):
            cp = ycopy(
                st1.at[c, pl.ds(i * hrow, hrow)],
                rv1.at[c, pl.ds(i * hrow, hrow)],
                rs_send.at[c, i],
                rs_recv.at[c, i],
                to,
            )
            cp.start()
            sends.append(cp)

        part[c, 0] = second(right)
        part[c, 1] = second(left)
        part[c, 2] = second(g)

    def stage_d(c):
        for i, to in enumerate((right, left)):
            a, b = i * hrow, (1 - i) * hrow
            arrived(rv1.at[c, pl.ds(a, hrow)], rs_recv.at[c, i])
            st2[c, i, a : a + hrow, :] = (
                part[c, i, a : a + hrow, :] + rv1[c, a : a + hrow, :].astype(F32)
            ).astype(BF16)
            st2[c, i, b : b + hrow, :] = part[c, i, b : b + hrow, :].astype(BF16)
            cp = ycopy(st2.at[c, i], rv2.at[c, i], rs_send.at[c, 2 + i], rs_recv.at[c, 2 + i], to)
            cp.start()
            sends.append(cp)

    def stage_e(c):
        for i in range(2):
            arrived(rv2.at[c, i], rs_recv.at[c, 2 + i])
        total = part[c, 2] + rv2[c, 0].astype(F32) + rv2[c, 1].astype(F32)
        total = total.reshape(per, CAPACITY, quarter)
        back[c] = jnp.concatenate([total[:, :, :half], total[:, :, half:]], axis=1).astype(BF16)

        def send(j, carry):
            z = (my_z + j) % per
            pltpu.make_async_remote_copy(
                src_ref=back.at[c, z],
                dst_ref=ybuf.at[d],
                send_sem=ret_send.at[c],
                recv_sem=ret_recv.at[c],
                device_id=(g, slab(c) + z),
                device_id_type=MESH,
            ).start()
            return carry

        if c == 0:
            pltpu.make_async_copy(back.at[0, my_z], ybuf.at[d], ret_recv.at[0]).start()
            lax.fori_loop(1, per, send, 0)
        else:
            lax.fori_loop(0, per, send, 0)

    stages = (stage_a, stage_b, stage_c, stage_d, stage_e)
    for step in range(n_x + len(stages) - 1):
        for k in reversed(range(len(stages))):
            if 0 <= step - k < n_x:
                stages[k](step - k)
        kv_event(step)

    kv_finish()
    columns_kv = wkv.shape[-1]
    heads = columns_kv // HEAD_DIM
    pairs = sent * heads
    row = lax.broadcasted_iota(jnp.int32, (pairs, columns_kv), 0)
    own_head = row % heads == lax.broadcasted_iota(jnp.int32, (pairs, columns_kv), 1) // HEAD_DIM
    query = jnp.zeros((pairs, columns_kv), F32)
    for i in range(sent):
        query = jnp.where(row // heads == i, query_ref[i : i + 1, :].astype(F32), query)
    query = jnp.where(own_head, query, 0.0).astype(BF16)

    def projection(kv):
        return wkv[:, :, kv].reshape(width, columns_kv)

    through = lax.dot_general(
        query, projection(0), (((1,), (1,)), ((), ())), preferred_element_type=F32
    )
    high = through.astype(BF16)
    qkey[:pairs, :] = high.astype(F32)
    qkey[pairs:, :] = through - high.astype(F32)

    acc = jnp.zeros((4 * rows, half), F32)
    for c in range(n_x):
        here = pl.ds(((my_x + c) % n_x) * per, per)
        arrived(ybuf.at[here], ret_recv.at[c])
        acc = acc + jnp.dot(
            combine[c], ybuf[here].reshape(mrow, half), preferred_element_type=F32
        )
    mix[g] = jnp.concatenate(
        [acc[:rows] + acc[rows : 2 * rows], acc[2 * rows : 3 * rows] + acc[3 * rows :]], axis=1
    ).astype(BF16)

    hm = rows // 2
    for i, to in enumerate((right, left)):
        cp = ycopy(mix.at[g], mix.at[g], mix_send.at[i], mix_recv.at[i], to)
        cp.start()
        sends.append(cp)
    for i, (origin, to) in enumerate(((left, right), (right, left))):
        arrived(mix.at[origin], mix_recv.at[i])
        piece = mix.at[origin, pl.ds(i * hm, hm)]
        cp = ycopy(piece, piece, mix_send.at[2 + i], mix_recv.at[2 + i], to)
        cp.start()
        sends.append(cp)
    for i in range(2):
        arrived(mix.at[diag, pl.ds(i * hm, hm)], mix_recv.at[2 + i])

    def final_block(i, carry):
        r = pl.ds(pl.multiple_of(i * blk, blk), blk)
        m = jnp.concatenate([mix[q, r, :] for q in range(4)], axis=1)
        v = enc_ref[r, :].astype(F32) + m.astype(F32)
        mean = jnp.mean(v, axis=-1, keepdims=True)
        cen = v - mean
        var = jnp.mean(cen * cen, axis=-1, keepdims=True)
        out_ref[r, :] = (cen * lax.rsqrt(var + EPSILON) * fgain_ref[...]).astype(BF16)
        return carry

    loads[6].wait()
    lax.fori_loop(0, rows // blk, final_block, 0)

    scores = lax.dot_general(
        qkey[...].astype(BF16), out_ref[...], (((1,), (1,)), ((), ())), preferred_element_type=F32
    )
    scores = (scores[:pairs] + scores[pairs:]) * (1.0 / math.sqrt(HEAD_DIM))
    which = lax.broadcasted_iota(jnp.int32, (pairs, rows), 0) // heads
    at = lax.broadcasted_iota(jnp.int32, (pairs, rows), 1)
    inside = jnp.zeros((pairs, rows), jnp.bool_)
    for i in range(sent):
        inside = inside | (
            (which == i) & (at >= i * length) & (at < i * length + lens_ref[i])
        )
    weights = jnp.where(inside, jnp.exp(scores), 0.0)
    probabilities = (weights / jnp.sum(weights, axis=-1, keepdims=True)).astype(BF16)
    mean_state = jnp.dot(probabilities, out_ref[...], preferred_element_type=F32)
    high = mean_state.astype(BF16)
    low = (mean_state - high.astype(F32)).astype(BF16)
    values = projection(1)
    context = jnp.dot(high, values, preferred_element_type=F32) + jnp.dot(
        low, values, preferred_element_type=F32
    )
    context = jnp.where(own_head, context, 0.0)
    for i in range(sent):
        context_ref[i : i + 1, :] = jnp.sum(
            jnp.where(row // heads == i, context, 0.0), axis=0, keepdims=True
        ).astype(BF16)

    for cp in sends + kv_sends:
        cp.wait_send()
    for c in range(n_x):
        count = per - 1 if c == 0 else per
        for buf, sem in ((dispatch, a2a_send), (back, ret_send)):
            arrived(buf.at[c, pl.ds(0, count)], sem.at[c])


def on_device(
    n_exp,
    enc_states,
    norm_gain,
    final_gain,
    expert_ids,
    expert_gates,
    source_lengths,
    w_in,
    w_out,
    w_key,
    w_value,
    cross_query,
):
    sent, length, width = enc_states.shape
    rows = sent * length
    n_x = 4 if n_exp > 16 else 16 // n_exp if n_exp < 16 else 1
    n_x = min(n_x, n_exp // 2)
    per = n_exp // n_x
    n_z = per // 2
    quarter, half = width // 4, width // 8
    crow, mrow = per * CAPACITY, per * 2 * CAPACITY
    ff = w_in.shape[2]
    kv_rows, kv_columns = w_key.shape
    pairs = sent * (kv_columns // HEAD_DIM)
    prow = -(-rows // 128) * 128
    vmem = pl.BlockSpec(memory_space=pltpu.VMEM)
    hbm = pl.BlockSpec(memory_space=pltpu.HBM)
    smem = pl.BlockSpec(memory_space=pltpu.SMEM)
    dma = pltpu.SemaphoreType.DMA
    encoded, context = pl.pallas_call(
        functools.partial(layer_kernel, n_exp, n_x),
        out_shape=(
            jax.ShapeDtypeStruct((rows, width), BF16),
            jax.ShapeDtypeStruct(cross_query.shape, BF16),
        ),
        in_specs=[smem, vmem, vmem, vmem] + [hbm] * 7,
        out_specs=(vmem, vmem),
        scratch_shapes=[
            pltpu.VMEM((rows, width), BF16),
            pltpu.VMEM((1, width), F32),
            pltpu.VMEM((1, width), F32),
            pltpu.VMEM((n_x, per, 2, kv_rows, kv_columns), BF16),
            pltpu.VMEM(w_in.shape[1:], BF16),
            pltpu.VMEM(w_out.shape[1:], BF16),
            pltpu.VMEM((2 * pairs, width), F32),
            pltpu.VMEM((prow, quarter), BF16),
            pltpu.VMEM((n_x, per, 2 * CAPACITY, half), BF16),
            pltpu.VMEM((4, n_exp, 2 * CAPACITY, half), BF16),
            pltpu.VMEM((n_x, 4 * rows, mrow), BF16),
            pltpu.VMEM((crow, width), BF16),
            pltpu.VMEM((crow, ff), BF16),
            pltpu.VMEM((n_x, 3, crow, quarter), F32),
            pltpu.VMEM((n_x, crow, quarter), BF16),
            pltpu.VMEM((n_x, crow, quarter), BF16),
            pltpu.VMEM((n_x, 2, crow, quarter), BF16),
            pltpu.VMEM((n_x, 2, crow, quarter), BF16),
            pltpu.VMEM((n_x, per, 2 * CAPACITY, half), BF16),
            pltpu.VMEM((n_exp, 2 * CAPACITY, half), BF16),
            pltpu.VMEM((4, rows, quarter), BF16),
            dma((7,)),
            dma((n_x,)),
            dma((n_x,)),
            dma((n_x, 4)),
            dma((n_x, 4)),
            dma((n_x, 4)),
            dma((n_x, 4)),
            dma((n_x,)),
            dma((n_x,)),
            dma((4,)),
            dma((4,)),
            dma((n_x,)),
            dma((n_x,)),
            dma((2, n_z // 2 + 1)),
            dma((2, n_z // 2 + 1)),
            dma((2, n_z // 2 + 1)),
            dma((2, n_z // 2 + 1)),
        ],
        compiler_params=pltpu.CompilerParams(
            collective_id=0, has_side_effects=True, vmem_limit_bytes=56 * 1024 * 1024
        ),
        cost_estimate=pl.CostEstimate(
            flops=4 * n_exp * CAPACITY * width * ff,
            bytes_accessed=12_000_000,
            transcendentals=0,
        ),
    )(
        source_lengths,
        expert_ids.transpose(0, 2, 1),
        expert_gates.transpose(0, 2, 1),
        cross_query,
        enc_states.reshape(rows, width),
        norm_gain.reshape(1, width),
        final_gain.reshape(1, width),
        w_key,
        w_value,
        w_in[0],
        w_out[0],
    )
    return encoded.reshape(sent, length, width), context


def solution(mesh):
    return jax.shard_map(
        functools.partial(on_device, mesh.shape["dev"]),
        mesh=mesh,
        in_specs=(
            P("dev", None, None),
            P(),
            P(),
            P("dev", None, None),
            P("dev", None, None),
            P("dev"),
            P("dev", None, "grp"),
            P("dev", "grp", None),
            P("dev", "grp"),
            P("dev", "grp"),
            P("dev", "grp"),
        ),
        out_specs=(P("dev", None, None), P("dev", "grp")),
        check_vma=False,
    )
```

```python
import functools
import math

import jax
import jax.numpy as jnp
from jax import lax
from jax.experimental import pallas as pl
from jax.experimental.pallas import tpu as pltpu
from jax.sharding import PartitionSpec as P

HEADS = 16
HEAD_DIM = 128
CAPACITY = 8
AHEAD = 3
ORDER = (
    ("a", 0), ("a", 1), ("k", 0), ("b", 0), ("a", 2), ("b", 1),
    ("a", 3), ("c", 0), ("b", 2), ("c", 1), ("d", 0), ("k", 1),
    ("b", 3), ("c", 2), ("d", 1), ("k", 2), ("e", 0), ("c", 3),
    ("d", 2), ("k", 3), ("e", 1), ("d", 3), ("e", 2), ("k", 4),
    ("e", 3),
)
EPSILON = 1e-05
F32 = jnp.float32
BF16 = jnp.bfloat16
MESH = pl.DeviceIdType.MESH


def layer_kernel(
    n_exp,
    n_x,
    lens_ref,
    ids_ref,
    gates_ref,
    query_ref,
    enc_hbm,
    ngain_hbm,
    fgain_hbm,
    wkey_hbm,
    wvalue_hbm,
    win_hbm,
    wout_hbm,
    out_ref,
    context_ref,
    enc_ref,
    ngain_ref,
    fgain_ref,
    wkv,
    win,
    wout,
    qkey,
    normed,
    dispatch,
    xbuf,
    combine,
    xrow,
    hid,
    part,
    st1,
    rv1,
    st2,
    rv2,
    back,
    ybuf,
    mix,
    w_sem,
    a2a_send,
    a2a_recv,
    yag_send,
    yag_recv,
    rs_send,
    rs_recv,
    ret_send,
    ret_recv,
    mix_send,
    mix_recv,
    kvx_send,
    kvx_recv,
    kvz_send,
    kvz_recv,
    kvc_send,
    kvc_recv,
):
    rows, width = enc_ref.shape
    sent, _, length = ids_ref.shape
    quarter = width // 4
    half = quarter // 2
    per = n_exp // n_x
    crow = per * CAPACITY
    mrow = per * 2 * CAPACITY
    prow = normed.shape[0]

    g = lax.axis_index("grp")
    d = lax.axis_index("dev")
    my_x = d // per
    my_z = d % per
    right, left, diag = (g + 1) % 4, (g + 3) % 4, (g + 2) % 4

    loads = [
        pltpu.make_async_copy(src, dst, w_sem.at[i])
        for i, (src, dst) in enumerate(
            (
                (enc_hbm, enc_ref),
                (ngain_hbm, ngain_ref),
                (wkey_hbm, wkv.at[my_x, my_z, 0]),
                (wvalue_hbm, wkv.at[my_x, my_z, 1]),
                (win_hbm, win),
                (wout_hbm, wout),
                (fgain_hbm, fgain_ref),
            )
        )
    ]
    for load in loads:
        load.start()

    barrier = pltpu.get_barrier_semaphore()

    def greet(i, carry):
        pl.semaphore_signal(barrier, inc=1, device_id=(g, (d + i) % n_exp), device_id_type=MESH)
        return carry

    lax.fori_loop(1, n_exp, greet, 0)
    for i in range(1, 4):
        pl.semaphore_signal(barrier, inc=1, device_id=((g + i) % 4, d), device_id_type=MESH)

    def arrived(ref, sem):
        pltpu.make_async_copy(ref, ref, sem).wait()

    loads[0].wait()
    loads[1].wait()

    blk = 16
    qcols = pl.ds(pl.multiple_of(g * quarter, 128), quarter)

    def norm_block(i, carry):
        r = pl.ds(pl.multiple_of(i * blk, blk), blk)
        v = enc_ref[r, :].astype(F32)
        mean = jnp.mean(v, axis=-1, keepdims=True)
        c = v - mean
        var = jnp.mean(c * c, axis=-1, keepdims=True)
        own = enc_ref[r, qcols].astype(F32) - mean
        own = own * lax.rsqrt(var + EPSILON) * ngain_ref[:, qcols]
        normed[r, :] = own.astype(BF16)
        return carry

    lax.fori_loop(0, rows // blk, norm_block, 0)
    if prow > rows:
        normed[rows:, :] = jnp.zeros((prow - rows, quarter), BF16)

    def along(ref, k):
        return jnp.concatenate([ref[i, k : k + 1, :] for i in range(sent)], axis=1)

    pos = lax.broadcasted_iota(jnp.int32, (1, rows), 1)
    live = jnp.zeros((1, rows), jnp.bool_)
    for i in range(sent):
        live = live | ((pos >= i * length) & (pos < i * length + lens_ref[i]))
    expert = lax.broadcasted_iota(jnp.int32, (n_exp, rows), 0)
    earlier = (
        lax.broadcasted_iota(jnp.int32, (rows, rows), 0)
        < lax.broadcasted_iota(jnp.int32, (rows, rows), 1)
    ).astype(BF16)
    codes = []
    offset = jnp.zeros((n_exp, 1), F32)
    for k in range(2):
        hot = jnp.where((along(ids_ref, k) == expert) & live, 1.0, 0.0).astype(F32)
        rank = jnp.dot(hot.astype(BF16), earlier, preferred_element_type=F32) + offset
        offset = offset + jnp.sum(hot, axis=1, keepdims=True)
        code = jnp.sum(
            hot * (rank + (2 * CAPACITY) * expert.astype(F32)), axis=0, keepdims=True
        )
        codes.append(jnp.where(live, code, -100.0))
    line = lax.broadcasted_iota(jnp.int32, (128, rows), 0)
    facts = jnp.zeros((128, rows), F32)
    for i, fact in enumerate(codes + [along(gates_ref, 0), along(gates_ref, 1)]):
        facts = jnp.where(line == i, fact, facts)
    if prow > rows:
        facts = jnp.concatenate([facts, jnp.zeros((128, prow - rows), F32)], axis=1)
        codes = [
            jnp.concatenate([v, jnp.full((1, prow - rows), -100.0, F32)], axis=1) for v in codes
        ]
    row0, row1 = codes[0].astype(jnp.int32), codes[1].astype(jnp.int32)
    columns = facts.T
    code0 = columns[:rows, 0:1].astype(jnp.int32)
    code1 = columns[:rows, 1:2].astype(jnp.int32)
    gate0, gate1 = columns[:rows, 2:3], columns[:rows, 3:4]

    for c in range(n_x):
        base = ((my_x + c) % n_x) * mrow
        r = lax.broadcasted_iota(jnp.int32, (mrow, prow), 0) + base
        acc = jnp.zeros((mrow, half), F32)
        for h in range(2):
            rh = r - h * CAPACITY
            pick = jnp.where((rh == row0) | (rh == row1), 1.0, 0.0).astype(BF16)
            acc = acc + jnp.dot(
                pick, normed[:, h * half : (h + 1) * half], preferred_element_type=F32
            )
        dispatch[c] = acc.astype(BF16).reshape(per, 2 * CAPACITY, half)

    pl.semaphore_wait(barrier, n_exp - 1 + 3)

    def dispatch_chunk(c):
        def send(j, carry):
            z = (my_z + j) % per
            pltpu.make_async_remote_copy(
                src_ref=dispatch.at[c, z],
                dst_ref=xbuf.at[g, d],
                send_sem=a2a_send.at[c],
                recv_sem=a2a_recv.at[c],
                device_id=(g, ((my_x + c) % n_x) * per + z),
                device_id_type=MESH,
            ).start()
            return carry

        if c == 0:
            pltpu.make_async_copy(
                dispatch.at[0, my_z], xbuf.at[g, d], a2a_recv.at[0]
            ).start()
            lax.fori_loop(1, per, send, 0)
        else:
            lax.fori_loop(0, per, send, 0)

    for c in range(min(AHEAD, n_x)):
        dispatch_chunk(c)

    n_z = per // 2
    my_zz, my_core = my_z // 2, my_z % 2
    kv_sends = []

    def kv_copy(ref, send_sem, recv_sem, to_x, to_z):
        cp = pltpu.make_async_remote_copy(
            src_ref=ref,
            dst_ref=ref,
            send_sem=send_sem,
            recv_sem=recv_sem,
            device_id=(g, to_x * per + to_z),
            device_id_type=MESH,
        )
        cp.start()
        kv_sends.append(cp)

    loads[2].wait()
    loads[3].wait()
    for i in range(1, n_x):
        kv_copy(
            wkv.at[my_x, my_z],
            kvx_send.at[i],
            kvx_recv.at[i],
            (my_x + i) % n_x,
            my_z,
        )

    def kv_piece(way, step, core):
        shift = step if way == 1 else n_z - step
        z = 2 * ((my_zz + shift) % n_z) + core
        if step < n_z // 2 or step == 0:
            return wkv.at[:, z]
        return wkv.at[:, z, way]

    def kv_event(step):
        if step > n_z // 2:
            return
        other = 2 * my_zz + (1 - my_core)
        if step == 0:
            for i in range(1, n_x):
                arrived(wkv.at[(my_x + n_x - i) % n_x, my_z], kvx_recv.at[i])
            kv_copy(kv_piece(0, 0, my_core), kvc_send.at[0, 0], kvc_recv.at[0, 0], my_x, other)
        for way in range(2):
            if step > 0:
                arrived(kv_piece(way, step, my_core), kvz_recv.at[way, step])
            if step < n_z // 2:
                ref = kv_piece(way, step, my_core)
                if step + 1 == n_z // 2:
                    shift = step if way == 1 else n_z - step
                    ref = wkv.at[:, 2 * ((my_zz + shift) % n_z) + my_core, way]
                to = 2 * ((my_zz + (1 if way == 0 else n_z - 1)) % n_z) + my_core
                kv_copy(ref, kvz_send.at[way, step], kvz_recv.at[way, step + 1], my_x, to)
            if step > 0:
                kv_copy(
                    kv_piece(way, step, my_core),
                    kvc_send.at[way, step],
                    kvc_recv.at[way, step],
                    my_x,
                    other,
                )

    def kv_finish():
        arrived(kv_piece(0, 0, 1 - my_core), kvc_recv.at[0, 0])
        for step in range(1, n_z // 2 + 1):
            for way in range(2):
                arrived(kv_piece(way, step, 1 - my_core), kvc_recv.at[way, step])

    for c in range(n_x):
        base = ((my_x + c) % n_x) * mrow
        col = lax.broadcasted_iota(jnp.int32, (rows, mrow), 1) + base
        for h in range(2):
            ch = col - h * CAPACITY
            value = jnp.where(ch == code0, gate0, jnp.where(ch == code1, gate1, 0.0))
            high = value.astype(BF16)
            combine[c, 2 * h * rows : (2 * h + 1) * rows, :] = high
            combine[c, (2 * h + 1) * rows : (2 * h + 2) * rows, :] = (
                value - high.astype(F32)
            ).astype(BF16)

    def slab(c):
        return ((my_x + n_x - c) % n_x) * per

    def ycopy(src, dst, send_sem, recv_sem, to):
        return pltpu.make_async_remote_copy(
            src_ref=src,
            dst_ref=dst,
            send_sem=send_sem,
            recv_sem=recv_sem,
            device_id=(to, d),
            device_id_type=MESH,
        )

    def xs(q, c, start=0, size=per):
        return xbuf.at[q, pl.ds(slab(c) + start, size)]

    hp = per // 2
    sends = []

    def stage_a(c):
        arrived(xs(g, c), a2a_recv.at[c])
        if c + AHEAD < n_x:
            dispatch_chunk(c + AHEAD)
        for i, to in enumerate((right, left)):
            cp = ycopy(xs(g, c), xs(g, c), yag_send.at[c, i], yag_recv.at[c, i], to)
            cp.start()
            sends.append(cp)

    def stage_b(c):
        arrived(xs(left, c), yag_recv.at[c, 0])
        cp = ycopy(
            xs(left, c, 0, hp), xs(left, c, 0, hp), yag_send.at[c, 2], yag_recv.at[c, 2], right
        )
        cp.start()
        sends.append(cp)
        arrived(xs(right, c), yag_recv.at[c, 1])
        cp = ycopy(
            xs(right, c, hp, hp), xs(right, c, hp, hp), yag_send.at[c, 3], yag_recv.at[c, 3], left
        )
        cp.start()
        sends.append(cp)

    hrow = crow // 2

    def stage_c(c):
        arrived(xs(diag, c, 0, hp), yag_recv.at[c, 2])
        arrived(xs(diag, c, hp, hp), yag_recv.at[c, 3])
        for q in range(4):
            block = xbuf[q, pl.ds(slab(c), per)].astype(F32)
            for h in range(2):
                xrow[:, q * quarter + h * half : q * quarter + (h + 1) * half] = (
                    block[:, h * CAPACITY : (h + 1) * CAPACITY, :]
                    .reshape(crow, half)
                    .astype(BF16)
                )
        if c == 0:
            loads[4].wait()
        tile = min(256, hid.shape[1])

        def first(n, carry):
            cs = pl.ds(pl.multiple_of(n * tile, tile), tile)
            hid[:, cs] = jnp.maximum(
                jnp.dot(xrow[...], win[:, cs], preferred_element_type=F32), 0.0
            ).astype(BF16)
            return carry

        lax.fori_loop(0, hid.shape[1] // tile, first, 0)
        if c == 0:
            loads[5].wait()

        def second(q):
            cs = pl.ds(pl.multiple_of(q * quarter, 128), quarter)
            return jnp.dot(hid[...], wout[:, cs], preferred_element_type=F32)

        st1[c] = second(diag).astype(BF16)
        for i, to in enumerate((right, left)):
            cp = ycopy(
                st1.at[c, pl.ds(i * hrow, hrow)],
                rv1.at[c, pl.ds(i * hrow, hrow)],
                rs_send.at[c, i],
                rs_recv.at[c, i],
                to,
            )
            cp.start()
            sends.append(cp)

        part[c, 0] = second(right)
        part[c, 1] = second(left)
        part[c, 2] = second(g)

    def stage_d(c):
        for i, to in enumerate((right, left)):
            a, b = i * hrow, (1 - i) * hrow
            arrived(rv1.at[c, pl.ds(a, hrow)], rs_recv.at[c, i])
            st2[c, i, a : a + hrow, :] = (
                part[c, i, a : a + hrow, :] + rv1[c, a : a + hrow, :].astype(F32)
            ).astype(BF16)
            st2[c, i, b : b + hrow, :] = part[c, i, b : b + hrow, :].astype(BF16)
            cp = ycopy(st2.at[c, i], rv2.at[c, i], rs_send.at[c, 2 + i], rs_recv.at[c, 2 + i], to)
            cp.start()
            sends.append(cp)

    def stage_e(c):
        for i in range(2):
            arrived(rv2.at[c, i], rs_recv.at[c, 2 + i])
        total = part[c, 2] + rv2[c, 0].astype(F32) + rv2[c, 1].astype(F32)
        total = total.reshape(per, CAPACITY, quarter)
        back[c] = jnp.concatenate([total[:, :, :half], total[:, :, half:]], axis=1).astype(BF16)

        def send(j, carry):
            z = (my_z + j) % per
            pltpu.make_async_remote_copy(
                src_ref=back.at[c, z],
                dst_ref=ybuf.at[d],
                send_sem=ret_send.at[c],
                recv_sem=ret_recv.at[c],
                device_id=(g, slab(c) + z),
                device_id_type=MESH,
            ).start()
            return carry

        if c == 0:
            pltpu.make_async_copy(back.at[0, my_z], ybuf.at[d], ret_recv.at[0]).start()
            lax.fori_loop(1, per, send, 0)
        else:
            lax.fori_loop(0, per, send, 0)

    stages = dict(a=stage_a, b=stage_b, c=stage_c, d=stage_d, e=stage_e, k=kv_event)
    for name, index in ORDER:
        if name == "k" or index < n_x:
            stages[name](index)

    kv_finish()
    columns_kv = wkv.shape[-1]
    heads = columns_kv // HEAD_DIM
    pairs = sent * heads
    row = lax.broadcasted_iota(jnp.int32, (pairs, columns_kv), 0)
    own_head = row % heads == lax.broadcasted_iota(jnp.int32, (pairs, columns_kv), 1) // HEAD_DIM
    query = jnp.zeros((pairs, columns_kv), F32)
    for i in range(sent):
        query = jnp.where(row // heads == i, query_ref[i : i + 1, :].astype(F32), query)
    query = jnp.where(own_head, query, 0.0).astype(BF16)

    def projection(kv):
        return wkv[:, :, kv].reshape(width, columns_kv)

    through = lax.dot_general(
        query, projection(0), (((1,), (1,)), ((), ())), preferred_element_type=F32
    )
    high = through.astype(BF16)
    qkey[:pairs, :] = high.astype(F32)
    qkey[pairs:, :] = through - high.astype(F32)

    acc = jnp.zeros((4 * rows, half), F32)
    for c in range(n_x):
        here = pl.ds(((my_x + c) % n_x) * per, per)
        arrived(ybuf.at[here], ret_recv.at[c])
        acc = acc + jnp.dot(
            combine[c], ybuf[here].reshape(mrow, half), preferred_element_type=F32
        )
    mix[g] = jnp.concatenate(
        [acc[:rows] + acc[rows : 2 * rows], acc[2 * rows : 3 * rows] + acc[3 * rows :]], axis=1
    ).astype(BF16)

    hm = rows // 2

    def mix_part(q, i):
        return mix.at[q, pl.ds(i * hm, hm)]

    for turn in range(2):
        for way, to in enumerate((right, left)):
            i = (way + turn) % 2
            cp = ycopy(
                mix_part(g, i), mix_part(g, i), mix_send.at[way, i], mix_recv.at[way, i], to
            )
            cp.start()
            sends.append(cp)
    for way, (origin, to) in enumerate(((left, right), (right, left))):
        arrived(mix_part(origin, way), mix_recv.at[way, way])
        cp = ycopy(
            mix_part(origin, way),
            mix_part(origin, way),
            mix_send.at[way, 2],
            mix_recv.at[way, 2],
            to,
        )
        cp.start()
        sends.append(cp)
    for way, origin in enumerate((left, right)):
        arrived(mix_part(origin, 1 - way), mix_recv.at[way, 1 - way])
    for way in range(2):
        arrived(mix_part(diag, way), mix_recv.at[way, 2])

    def final_block(i, carry):
        r = pl.ds(pl.multiple_of(i * blk, blk), blk)
        m = jnp.concatenate([mix[q, r, :] for q in range(4)], axis=1)
        v = enc_ref[r, :].astype(F32) + m.astype(F32)
        mean = jnp.mean(v, axis=-1, keepdims=True)
        cen = v - mean
        var = jnp.mean(cen * cen, axis=-1, keepdims=True)
        out_ref[r, :] = (cen * lax.rsqrt(var + EPSILON) * fgain_ref[...]).astype(BF16)
        return carry

    loads[6].wait()
    lax.fori_loop(0, rows // blk, final_block, 0, unroll=2)

    scores = lax.dot_general(
        qkey[...].astype(BF16), out_ref[...], (((1,), (1,)), ((), ())), preferred_element_type=F32
    )
    scores = (scores[:pairs] + scores[pairs:]) * (1.0 / math.sqrt(HEAD_DIM))
    which = lax.broadcasted_iota(jnp.int32, (pairs, rows), 0) // heads
    at = lax.broadcasted_iota(jnp.int32, (pairs, rows), 1)
    inside = jnp.zeros((pairs, rows), jnp.bool_)
    for i in range(sent):
        inside = inside | (
            (which == i) & (at >= i * length) & (at < i * length + lens_ref[i])
        )
    weights = jnp.where(inside, jnp.exp(scores), 0.0)
    probabilities = (weights / jnp.sum(weights, axis=-1, keepdims=True)).astype(BF16)
    mean_state = jnp.dot(probabilities, out_ref[...], preferred_element_type=F32)
    high = mean_state.astype(BF16)
    low = (mean_state - high.astype(F32)).astype(BF16)
    values = projection(1)
    context = jnp.dot(high, values, preferred_element_type=F32) + jnp.dot(
        low, values, preferred_element_type=F32
    )
    context = jnp.where(own_head, context, 0.0)
    for i in range(sent):
        context_ref[i : i + 1, :] = jnp.sum(
            jnp.where(row // heads == i, context, 0.0), axis=0, keepdims=True
        ).astype(BF16)

    for cp in sends + kv_sends:
        cp.wait_send()
    for c in range(n_x):
        count = per - 1 if c == 0 else per
        for buf, sem in ((dispatch, a2a_send), (back, ret_send)):
            arrived(buf.at[c, pl.ds(0, count)], sem.at[c])


def in_hbm(array):
    return pltpu.with_memory_space_constraint(array, pltpu.HBM)


def on_device(
    n_exp,
    enc_states,
    norm_gain,
    final_gain,
    expert_ids,
    expert_gates,
    source_lengths,
    w_in,
    w_out,
    w_key,
    w_value,
    cross_query,
):
    sent, length, width = enc_states.shape
    rows = sent * length
    n_x = 1 if n_exp == 16 else min(4, n_exp // 2)
    per = n_exp // n_x
    n_z = per // 2
    quarter, half = width // 4, width // 8
    crow, mrow = per * CAPACITY, per * 2 * CAPACITY
    ff = w_in.shape[2]
    kv_rows, kv_columns = w_key.shape
    pairs = sent * (kv_columns // HEAD_DIM)
    prow = -(-rows // 128) * 128
    vmem = pl.BlockSpec(memory_space=pltpu.VMEM)
    hbm = pl.BlockSpec(memory_space=pltpu.HBM)
    smem = pl.BlockSpec(memory_space=pltpu.SMEM)
    dma = pltpu.SemaphoreType.DMA
    encoded, context = pl.pallas_call(
        functools.partial(layer_kernel, n_exp, n_x),
        out_shape=(
            jax.ShapeDtypeStruct((rows, width), BF16),
            jax.ShapeDtypeStruct(cross_query.shape, BF16),
        ),
        in_specs=[smem, vmem, vmem, vmem] + [hbm] * 7,
        out_specs=(vmem, vmem),
        scratch_shapes=[
            pltpu.VMEM((rows, width), BF16),
            pltpu.VMEM((1, width), F32),
            pltpu.VMEM((1, width), F32),
            pltpu.VMEM((n_x, per, 2, kv_rows, kv_columns), BF16),
            pltpu.VMEM(w_in.shape[1:], BF16),
            pltpu.VMEM(w_out.shape[1:], BF16),
            pltpu.VMEM((2 * pairs, width), F32),
            pltpu.VMEM((prow, quarter), BF16),
            pltpu.VMEM((n_x, per, 2 * CAPACITY, half), BF16),
            pltpu.VMEM((4, n_exp, 2 * CAPACITY, half), BF16),
            pltpu.VMEM((n_x, 4 * rows, mrow), BF16),
            pltpu.VMEM((crow, width), BF16),
            pltpu.VMEM((crow, ff), BF16),
            pltpu.VMEM((n_x, 3, crow, quarter), F32),
            pltpu.VMEM((n_x, crow, quarter), BF16),
            pltpu.VMEM((n_x, crow, quarter), BF16),
            pltpu.VMEM((n_x, 2, crow, quarter), BF16),
            pltpu.VMEM((n_x, 2, crow, quarter), BF16),
            pltpu.VMEM((n_x, per, 2 * CAPACITY, half), BF16),
            pltpu.VMEM((n_exp, 2 * CAPACITY, half), BF16),
            pltpu.VMEM((4, rows, quarter), BF16),
            dma((7,)),
            dma((n_x,)),
            dma((n_x,)),
            dma((n_x, 4)),
            dma((n_x, 4)),
            dma((n_x, 4)),
            dma((n_x, 4)),
            dma((n_x,)),
            dma((n_x,)),
            dma((2, 3)),
            dma((2, 3)),
            dma((n_x,)),
            dma((n_x,)),
            dma((2, n_z // 2 + 1)),
            dma((2, n_z // 2 + 1)),
            dma((2, n_z // 2 + 1)),
            dma((2, n_z // 2 + 1)),
        ],
        compiler_params=pltpu.CompilerParams(
            collective_id=0, has_side_effects=True, vmem_limit_bytes=40 * 1024 * 1024
        ),
        cost_estimate=pl.CostEstimate(
            flops=4 * n_exp * CAPACITY * width * ff,
            bytes_accessed=12_000_000,
            transcendentals=0,
        ),
    )(
        in_hbm(source_lengths),
        in_hbm(expert_ids.transpose(0, 2, 1)),
        in_hbm(expert_gates.transpose(0, 2, 1)),
        in_hbm(cross_query),
        in_hbm(enc_states.reshape(rows, width)),
        in_hbm(norm_gain.reshape(1, width)),
        in_hbm(final_gain.reshape(1, width)),
        in_hbm(w_key),
        in_hbm(w_value),
        in_hbm(w_in[0]),
        in_hbm(w_out[0]),
    )
    return encoded.reshape(sent, length, width), context


def solution(mesh):
    return jax.shard_map(
        functools.partial(on_device, mesh.shape["dev"]),
        mesh=mesh,
        in_specs=(
            P("dev", None, None),
            P(),
            P(),
            P("dev", None, None),
            P("dev", None, None),
            P("dev"),
            P("dev", None, "grp"),
            P("dev", "grp", None),
            P("dev", "grp"),
            P("dev", "grp"),
            P("dev", "grp"),
        ),
        out_specs=(P("dev", None, None), P("dev", "grp")),
        check_vma=False,
    )
```

```python
import functools
import math

import jax
import jax.numpy as jnp
from jax import lax
from jax.experimental import pallas as pl
from jax.experimental.pallas import tpu as pltpu
from jax.sharding import PartitionSpec as P

HEADS = 16
HEAD_DIM = 128
CAPACITY = 8
AHEAD = 3
UNROLL = 6
ORDER = (
    ("a", 0), ("a", 1), ("k", 0), ("b", 0), ("a", 2), ("p", 0),
    ("b", 1), ("a", 3), ("c", 0), ("p", 1), ("b", 2), ("c", 1),
    ("p", 2), ("d", 0), ("k", 1), ("b", 3), ("c", 2), ("p", 3),
    ("d", 1), ("k", 2), ("e", 0), ("c", 3), ("d", 2), ("k", 3),
    ("e", 1), ("d", 3), ("e", 2), ("k", 4), ("e", 3),
)
EPSILON = 1e-05
F32 = jnp.float32
BF16 = jnp.bfloat16
MESH = pl.DeviceIdType.MESH


def layer_kernel(
    n_exp,
    n_x,
    lens_ref,
    ids_ref,
    gates_ref,
    query_ref,
    enc_hbm,
    ngain_hbm,
    fgain_hbm,
    wkey_hbm,
    wvalue_hbm,
    win_hbm,
    wout_hbm,
    out_ref,
    context_ref,
    enc_ref,
    ngain_ref,
    fgain_ref,
    wkv,
    win,
    wout,
    qkey,
    normed,
    dispatch,
    xbuf,
    combine,
    xrow,
    hid,
    hidden_sum,
    part,
    st1,
    rv1,
    st2,
    rv2,
    back,
    ybuf,
    mix,
    w_sem,
    a2a_send,
    a2a_recv,
    yag_send,
    yag_recv,
    rs_send,
    rs_recv,
    ret_send,
    ret_recv,
    mix_send,
    mix_recv,
    kvx_send,
    kvx_recv,
    kvz_send,
    kvz_recv,
    kvc_send,
    kvc_recv,
):
    rows, width = enc_ref.shape
    sent, _, length = ids_ref.shape
    quarter = width // 4
    half = quarter // 2
    per = n_exp // n_x
    crow = per * CAPACITY
    mrow = per * 2 * CAPACITY
    prow = normed.shape[0]

    g = lax.axis_index("grp")
    d = lax.axis_index("dev")
    my_x = d // per
    my_z = d % per
    right, left, diag = (g + 1) % 4, (g + 3) % 4, (g + 2) % 4

    loads = [
        pltpu.make_async_copy(src, dst, w_sem.at[i])
        for i, (src, dst) in enumerate(
            (
                (enc_hbm, enc_ref),
                (ngain_hbm, ngain_ref),
                (wkey_hbm, wkv.at[my_x, my_z, 0]),
                (wvalue_hbm, wkv.at[my_x, my_z, 1]),
                (win_hbm, win),
                (wout_hbm, wout),
                (fgain_hbm, fgain_ref),
            )
        )
    ]
    for load in loads:
        load.start()

    barrier = pltpu.get_barrier_semaphore()

    def greet(i, carry):
        pl.semaphore_signal(barrier, inc=1, device_id=(g, (d + i) % n_exp), device_id_type=MESH)
        return carry

    lax.fori_loop(1, n_exp, greet, 0)
    for i in range(1, 4):
        pl.semaphore_signal(barrier, inc=1, device_id=((g + i) % 4, d), device_id_type=MESH)

    def arrived(ref, sem):
        pltpu.make_async_copy(ref, ref, sem).wait()

    loads[0].wait()
    loads[1].wait()

    blk = 16
    qcols = pl.ds(pl.multiple_of(g * quarter, 128), quarter)

    def norm_block(i, carry):
        r = pl.ds(pl.multiple_of(i * blk, blk), blk)
        v = enc_ref[r, :].astype(F32)
        mean = jnp.mean(v, axis=-1, keepdims=True)
        c = v - mean
        var = jnp.mean(c * c, axis=-1, keepdims=True)
        own = enc_ref[r, qcols].astype(F32) - mean
        own = own * lax.rsqrt(var + EPSILON) * ngain_ref[:, qcols]
        normed[r, :] = own.astype(BF16)
        return carry

    lax.fori_loop(0, rows // blk, norm_block, 0)
    if prow > rows:
        normed[rows:, :] = jnp.zeros((prow - rows, quarter), BF16)

    def along(ref, k):
        return jnp.concatenate([ref[i, k : k + 1, :] for i in range(sent)], axis=1)

    pos = lax.broadcasted_iota(jnp.int32, (1, rows), 1)
    live = jnp.zeros((1, rows), jnp.bool_)
    for i in range(sent):
        live = live | ((pos >= i * length) & (pos < i * length + lens_ref[i]))
    expert = lax.broadcasted_iota(jnp.int32, (n_exp, rows), 0)
    earlier = (
        lax.broadcasted_iota(jnp.int32, (rows, rows), 0)
        < lax.broadcasted_iota(jnp.int32, (rows, rows), 1)
    ).astype(BF16)
    codes = []
    offset = jnp.zeros((n_exp, 1), F32)
    for k in range(2):
        hot = jnp.where((along(ids_ref, k) == expert) & live, 1.0, 0.0).astype(F32)
        rank = jnp.dot(hot.astype(BF16), earlier, preferred_element_type=F32) + offset
        offset = offset + jnp.sum(hot, axis=1, keepdims=True)
        code = jnp.sum(
            hot * (rank + (2 * CAPACITY) * expert.astype(F32)), axis=0, keepdims=True
        )
        codes.append(jnp.where(live, code, -100.0))
    line = lax.broadcasted_iota(jnp.int32, (128, rows), 0)
    facts = jnp.zeros((128, rows), F32)
    for i, fact in enumerate(codes + [along(gates_ref, 0), along(gates_ref, 1)]):
        facts = jnp.where(line == i, fact, facts)
    if prow > rows:
        facts = jnp.concatenate([facts, jnp.zeros((128, prow - rows), F32)], axis=1)
        codes = [
            jnp.concatenate([v, jnp.full((1, prow - rows), -100.0, F32)], axis=1) for v in codes
        ]
    row0, row1 = codes[0].astype(jnp.int32), codes[1].astype(jnp.int32)
    columns = facts.T
    code0 = columns[:rows, 0:1].astype(jnp.int32)
    code1 = columns[:rows, 1:2].astype(jnp.int32)
    gate0, gate1 = columns[:rows, 2:3], columns[:rows, 3:4]

    for c in range(n_x):
        base = ((my_x + c) % n_x) * mrow
        r = lax.broadcasted_iota(jnp.int32, (mrow, prow), 0) + base
        acc = jnp.zeros((mrow, half), F32)
        for h in range(2):
            rh = r - h * CAPACITY
            pick = jnp.where((rh == row0) | (rh == row1), 1.0, 0.0).astype(BF16)
            acc = acc + jnp.dot(
                pick, normed[:, h * half : (h + 1) * half], preferred_element_type=F32
            )
        dispatch[c] = acc.astype(BF16).reshape(per, 2 * CAPACITY, half)

    pl.semaphore_wait(barrier, n_exp - 1 + 3)

    def dispatch_chunk(c):
        def send(j, carry):
            z = (my_z + j) % per
            pltpu.make_async_remote_copy(
                src_ref=dispatch.at[c, z],
                dst_ref=xbuf.at[g, d],
                send_sem=a2a_send.at[c],
                recv_sem=a2a_recv.at[c],
                device_id=(g, ((my_x + c) % n_x) * per + z),
                device_id_type=MESH,
            ).start()
            return carry

        if c == 0:
            pltpu.make_async_copy(
                dispatch.at[0, my_z], xbuf.at[g, d], a2a_recv.at[0]
            ).start()
            lax.fori_loop(1, per, send, 0)
        else:
            lax.fori_loop(0, per, send, 0)

    for c in range(min(AHEAD, n_x)):
        dispatch_chunk(c)

    n_z = per // 2
    my_zz, my_core = my_z // 2, my_z % 2
    kv_sends = []

    def kv_copy(ref, send_sem, recv_sem, to_x, to_z):
        cp = pltpu.make_async_remote_copy(
            src_ref=ref,
            dst_ref=ref,
            send_sem=send_sem,
            recv_sem=recv_sem,
            device_id=(g, to_x * per + to_z),
            device_id_type=MESH,
        )
        cp.start()
        kv_sends.append(cp)

    loads[2].wait()
    loads[3].wait()
    for i in range(1, n_x):
        kv_copy(
            wkv.at[my_x, my_z],
            kvx_send.at[i],
            kvx_recv.at[i],
            (my_x + i) % n_x,
            my_z,
        )

    def kv_piece(way, step, core):
        shift = step if way == 1 else n_z - step
        z = 2 * ((my_zz + shift) % n_z) + core
        if step < n_z // 2 or step == 0:
            return wkv.at[:, z]
        return wkv.at[:, z, way]

    def kv_event(step):
        if step > n_z // 2:
            return
        other = 2 * my_zz + (1 - my_core)
        if step == 0:
            for i in range(1, n_x):
                arrived(wkv.at[(my_x + n_x - i) % n_x, my_z], kvx_recv.at[i])
            kv_copy(kv_piece(0, 0, my_core), kvc_send.at[0, 0], kvc_recv.at[0, 0], my_x, other)
        for way in range(2):
            if step > 0:
                arrived(kv_piece(way, step, my_core), kvz_recv.at[way, step])
            if step < n_z // 2:
                ref = kv_piece(way, step, my_core)
                if step + 1 == n_z // 2:
                    shift = step if way == 1 else n_z - step
                    ref = wkv.at[:, 2 * ((my_zz + shift) % n_z) + my_core, way]
                to = 2 * ((my_zz + (1 if way == 0 else n_z - 1)) % n_z) + my_core
                kv_copy(ref, kvz_send.at[way, step], kvz_recv.at[way, step + 1], my_x, to)
            if step > 0:
                kv_copy(
                    kv_piece(way, step, my_core),
                    kvc_send.at[way, step],
                    kvc_recv.at[way, step],
                    my_x,
                    other,
                )

    def kv_finish():
        arrived(kv_piece(0, 0, 1 - my_core), kvc_recv.at[0, 0])
        for step in range(1, n_z // 2 + 1):
            for way in range(2):
                arrived(kv_piece(way, step, 1 - my_core), kvc_recv.at[way, step])

    for c in range(n_x):
        base = ((my_x + c) % n_x) * mrow
        col = lax.broadcasted_iota(jnp.int32, (rows, mrow), 1) + base
        for h in range(2):
            ch = col - h * CAPACITY
            value = jnp.where(ch == code0, gate0, jnp.where(ch == code1, gate1, 0.0))
            high = value.astype(BF16)
            combine[c, 2 * h * rows : (2 * h + 1) * rows, :] = high
            combine[c, (2 * h + 1) * rows : (2 * h + 2) * rows, :] = (
                value - high.astype(F32)
            ).astype(BF16)

    def slab(c):
        return ((my_x + n_x - c) % n_x) * per

    def ycopy(src, dst, send_sem, recv_sem, to):
        return pltpu.make_async_remote_copy(
            src_ref=src,
            dst_ref=dst,
            send_sem=send_sem,
            recv_sem=recv_sem,
            device_id=(to, d),
            device_id_type=MESH,
        )

    def xs(q, c, start=0, size=per):
        return xbuf.at[q, pl.ds(slab(c) + start, size)]

    hp = per // 2
    sends = []

    def stage_a(c):
        arrived(xs(g, c), a2a_recv.at[c])
        if c + AHEAD < n_x:
            dispatch_chunk(c + AHEAD)
        for i, to in enumerate((right, left)):
            cp = ycopy(xs(g, c), xs(g, c), yag_send.at[c, i], yag_recv.at[c, i], to)
            cp.start()
            sends.append(cp)

    def stage_b(c):
        arrived(xs(left, c), yag_recv.at[c, 0])
        cp = ycopy(
            xs(left, c, 0, hp), xs(left, c, 0, hp), yag_send.at[c, 2], yag_recv.at[c, 2], right
        )
        cp.start()
        sends.append(cp)
        arrived(xs(right, c), yag_recv.at[c, 1])
        cp = ycopy(
            xs(right, c, hp, hp), xs(right, c, hp, hp), yag_send.at[c, 3], yag_recv.at[c, 3], left
        )
        cp.start()
        sends.append(cp)

    hrow = crow // 2

    tile = min(256, hid.shape[1])

    def place(k, q, c):
        block = xbuf[q, pl.ds(slab(c), per)].astype(F32)
        for h in range(2):
            xrow[:, k * quarter + h * half : k * quarter + (h + 1) * half] = (
                block[:, h * CAPACITY : (h + 1) * CAPACITY, :].reshape(crow, half).astype(BF16)
            )

    def term(k, q, cs):
        features = pl.ds(pl.multiple_of(q * quarter, 128), quarter)
        return jnp.dot(
            xrow[:, k * quarter : (k + 1) * quarter],
            win[features, cs],
            preferred_element_type=F32,
        )

    def stage_p(c):
        if c == 0:
            loads[4].wait()
        early = (g, left, right)
        for k, q in enumerate(early):
            place(k, q, c)

        def add_early(n, carry):
            cs = pl.ds(pl.multiple_of(n * tile, tile), tile)
            hidden_sum[c, :, cs] = term(0, g, cs) + term(1, left, cs) + term(2, right, cs)
            return carry

        lax.fori_loop(0, hid.shape[1] // tile, add_early, 0)

    def stage_c(c):
        arrived(xs(diag, c, 0, hp), yag_recv.at[c, 2])
        arrived(xs(diag, c, hp, hp), yag_recv.at[c, 3])
        place(3, diag, c)

        def add_last(n, carry):
            cs = pl.ds(pl.multiple_of(n * tile, tile), tile)
            total = hidden_sum[c, :, cs] + term(3, diag, cs)
            hid[:, cs] = jnp.maximum(total, 0.0).astype(BF16)
            return carry

        lax.fori_loop(0, hid.shape[1] // tile, add_last, 0)
        if c == 0:
            loads[5].wait()

        def second(q):
            cs = pl.ds(pl.multiple_of(q * quarter, 128), quarter)
            return jnp.dot(hid[...], wout[:, cs], preferred_element_type=F32)

        st1[c] = second(diag).astype(BF16)
        for i, to in enumerate((right, left)):
            cp = ycopy(
                st1.at[c, pl.ds(i * hrow, hrow)],
                rv1.at[c, pl.ds(i * hrow, hrow)],
                rs_send.at[c, i],
                rs_recv.at[c, i],
                to,
            )
            cp.start()
            sends.append(cp)

        part[c, 0] = second(right)
        part[c, 1] = second(left)
        part[c, 2] = second(g)

    def stage_d(c):
        for i, to in enumerate((right, left)):
            a, b = i * hrow, (1 - i) * hrow
            arrived(rv1.at[c, pl.ds(a, hrow)], rs_recv.at[c, i])
            st2[c, i, a : a + hrow, :] = (
                part[c, i, a : a + hrow, :] + rv1[c, a : a + hrow, :].astype(F32)
            ).astype(BF16)
            st2[c, i, b : b + hrow, :] = part[c, i, b : b + hrow, :].astype(BF16)
            cp = ycopy(st2.at[c, i], rv2.at[c, i], rs_send.at[c, 2 + i], rs_recv.at[c, 2 + i], to)
            cp.start()
            sends.append(cp)

    def stage_e(c):
        for i in range(2):
            arrived(rv2.at[c, i], rs_recv.at[c, 2 + i])
        total = part[c, 2] + rv2[c, 0].astype(F32) + rv2[c, 1].astype(F32)
        total = total.reshape(per, CAPACITY, quarter)
        back[c] = jnp.concatenate([total[:, :, :half], total[:, :, half:]], axis=1).astype(BF16)

        def send(j, carry):
            z = (my_z + j) % per
            pltpu.make_async_remote_copy(
                src_ref=back.at[c, z],
                dst_ref=ybuf.at[d],
                send_sem=ret_send.at[c],
                recv_sem=ret_recv.at[c],
                device_id=(g, slab(c) + z),
                device_id_type=MESH,
            ).start()
            return carry

        if c == 0:
            pltpu.make_async_copy(back.at[0, my_z], ybuf.at[d], ret_recv.at[0]).start()
            lax.fori_loop(1, per, send, 0)
        else:
            lax.fori_loop(0, per, send, 0)

    stages = dict(p=stage_p, a=stage_a, b=stage_b, c=stage_c, d=stage_d, e=stage_e, k=kv_event)
    for name, index in ORDER:
        if name == "k" or index < n_x:
            stages[name](index)

    kv_finish()
    columns_kv = wkv.shape[-1]
    heads = columns_kv // HEAD_DIM
    pairs = sent * heads
    row = lax.broadcasted_iota(jnp.int32, (pairs, columns_kv), 0)
    own_head = row % heads == lax.broadcasted_iota(jnp.int32, (pairs, columns_kv), 1) // HEAD_DIM
    query = jnp.zeros((pairs, columns_kv), F32)
    for i in range(sent):
        query = jnp.where(row // heads == i, query_ref[i : i + 1, :].astype(F32), query)
    query = jnp.where(own_head, query, 0.0).astype(BF16)

    def projection(kv):
        return wkv[:, :, kv].reshape(width, columns_kv)

    through = lax.dot_general(
        query, projection(0), (((1,), (1,)), ((), ())), preferred_element_type=F32
    )
    high = through.astype(BF16)
    qkey[:pairs, :] = high.astype(F32)
    qkey[pairs:, :] = through - high.astype(F32)

    acc = jnp.zeros((4 * rows, half), F32)
    for c in range(n_x):
        here = pl.ds(((my_x + c) % n_x) * per, per)
        arrived(ybuf.at[here], ret_recv.at[c])
        acc = acc + jnp.dot(
            combine[c], ybuf[here].reshape(mrow, half), preferred_element_type=F32
        )
    mix[g] = jnp.concatenate(
        [acc[:rows] + acc[rows : 2 * rows], acc[2 * rows : 3 * rows] + acc[3 * rows :]], axis=1
    ).astype(BF16)

    hm = rows // 2

    def mix_part(q, i):
        return mix.at[q, pl.ds(i * hm, hm)]

    for turn in range(2):
        for way, to in enumerate((right, left)):
            i = (way + turn) % 2
            cp = ycopy(
                mix_part(g, i), mix_part(g, i), mix_send.at[way, i], mix_recv.at[way, i], to
            )
            cp.start()
            sends.append(cp)
    for way, (origin, to) in enumerate(((left, right), (right, left))):
        arrived(mix_part(origin, way), mix_recv.at[way, way])
        cp = ycopy(
            mix_part(origin, way),
            mix_part(origin, way),
            mix_send.at[way, 2],
            mix_recv.at[way, 2],
            to,
        )
        cp.start()
        sends.append(cp)
    for way, origin in enumerate((left, right)):
        arrived(mix_part(origin, 1 - way), mix_recv.at[way, 1 - way])
    for way in range(2):
        arrived(mix_part(diag, way), mix_recv.at[way, 2])

    def final_block(i, carry):
        r = pl.ds(pl.multiple_of(i * blk, blk), blk)
        m = jnp.concatenate([mix[q, r, :] for q in range(4)], axis=1)
        v = enc_ref[r, :].astype(F32) + m.astype(F32)
        mean = jnp.mean(v, axis=-1, keepdims=True)
        cen = v - mean
        var = jnp.mean(cen * cen, axis=-1, keepdims=True)
        out_ref[r, :] = (cen * lax.rsqrt(var + EPSILON) * fgain_ref[...]).astype(BF16)
        return carry

    loads[6].wait()
    lax.fori_loop(0, rows // blk, final_block, 0, unroll=UNROLL)

    scores = lax.dot_general(
        qkey[...].astype(BF16), out_ref[...], (((1,), (1,)), ((), ())), preferred_element_type=F32
    )
    scores = (scores[:pairs] + scores[pairs:]) * (1.0 / math.sqrt(HEAD_DIM))
    which = lax.broadcasted_iota(jnp.int32, (pairs, rows), 0) // heads
    at = lax.broadcasted_iota(jnp.int32, (pairs, rows), 1)
    inside = jnp.zeros((pairs, rows), jnp.bool_)
    for i in range(sent):
        inside = inside | (
            (which == i) & (at >= i * length) & (at < i * length + lens_ref[i])
        )
    weights = jnp.where(inside, jnp.exp(scores), 0.0)
    probabilities = (weights / jnp.sum(weights, axis=-1, keepdims=True)).astype(BF16)
    mean_state = jnp.dot(probabilities, out_ref[...], preferred_element_type=F32)
    high = mean_state.astype(BF16)
    low = (mean_state - high.astype(F32)).astype(BF16)
    terms = jnp.dot(
        jnp.concatenate([high, low], axis=0), projection(1), preferred_element_type=F32
    )
    context = jnp.where(own_head, terms[:pairs] + terms[pairs:], 0.0)
    for i in range(sent):
        context_ref[i : i + 1, :] = jnp.sum(
            jnp.where(row // heads == i, context, 0.0), axis=0, keepdims=True
        ).astype(BF16)

    for cp in sends + kv_sends:
        cp.wait_send()
    for c in range(n_x):
        count = per - 1 if c == 0 else per
        for buf, sem in ((dispatch, a2a_send), (back, ret_send)):
            arrived(buf.at[c, pl.ds(0, count)], sem.at[c])


def in_hbm(array):
    return pltpu.with_memory_space_constraint(array, pltpu.HBM)


def on_device(
    n_exp,
    enc_states,
    norm_gain,
    final_gain,
    expert_ids,
    expert_gates,
    source_lengths,
    w_in,
    w_out,
    w_key,
    w_value,
    cross_query,
):
    sent, length, width = enc_states.shape
    rows = sent * length
    n_x = 1 if n_exp == 16 else min(4, n_exp // 2)
    per = n_exp // n_x
    n_z = per // 2
    quarter, half = width // 4, width // 8
    crow, mrow = per * CAPACITY, per * 2 * CAPACITY
    ff = w_in.shape[2]
    kv_rows, kv_columns = w_key.shape
    pairs = sent * (kv_columns // HEAD_DIM)
    prow = -(-rows // 128) * 128
    vmem = pl.BlockSpec(memory_space=pltpu.VMEM)
    hbm = pl.BlockSpec(memory_space=pltpu.HBM)
    smem = pl.BlockSpec(memory_space=pltpu.SMEM)
    dma = pltpu.SemaphoreType.DMA
    encoded, context = pl.pallas_call(
        functools.partial(layer_kernel, n_exp, n_x),
        out_shape=(
            jax.ShapeDtypeStruct((rows, width), BF16),
            jax.ShapeDtypeStruct(cross_query.shape, BF16),
        ),
        in_specs=[smem, vmem, vmem, vmem] + [hbm] * 7,
        out_specs=(vmem, vmem),
        scratch_shapes=[
            pltpu.VMEM((rows, width), BF16),
            pltpu.VMEM((1, width), F32),
            pltpu.VMEM((1, width), F32),
            pltpu.VMEM((n_x, per, 2, kv_rows, kv_columns), BF16),
            pltpu.VMEM(w_in.shape[1:], BF16),
            pltpu.VMEM(w_out.shape[1:], BF16),
            pltpu.VMEM((2 * pairs, width), F32),
            pltpu.VMEM((prow, quarter), BF16),
            pltpu.VMEM((n_x, per, 2 * CAPACITY, half), BF16),
            pltpu.VMEM((4, n_exp, 2 * CAPACITY, half), BF16),
            pltpu.VMEM((n_x, 4 * rows, mrow), BF16),
            pltpu.VMEM((crow, width), BF16),
            pltpu.VMEM((crow, ff), BF16),
            pltpu.VMEM((n_x, crow, ff), F32),
            pltpu.VMEM((n_x, 3, crow, quarter), F32),
            pltpu.VMEM((n_x, crow, quarter), BF16),
            pltpu.VMEM((n_x, crow, quarter), BF16),
            pltpu.VMEM((n_x, 2, crow, quarter), BF16),
            pltpu.VMEM((n_x, 2, crow, quarter), BF16),
            pltpu.VMEM((n_x, per, 2 * CAPACITY, half), BF16),
            pltpu.VMEM((n_exp, 2 * CAPACITY, half), BF16),
            pltpu.VMEM((4, rows, quarter), BF16),
            dma((7,)),
            dma((n_x,)),
            dma((n_x,)),
            dma((n_x, 4)),
            dma((n_x, 4)),
            dma((n_x, 4)),
            dma((n_x, 4)),
            dma((n_x,)),
            dma((n_x,)),
            dma((2, 3)),
            dma((2, 3)),
            dma((n_x,)),
            dma((n_x,)),
            dma((2, n_z // 2 + 1)),
            dma((2, n_z // 2 + 1)),
            dma((2, n_z // 2 + 1)),
            dma((2, n_z // 2 + 1)),
        ],
        compiler_params=pltpu.CompilerParams(
            collective_id=0, has_side_effects=True, vmem_limit_bytes=40 * 1024 * 1024
        ),
        cost_estimate=pl.CostEstimate(
            flops=4 * n_exp * CAPACITY * width * ff,
            bytes_accessed=12_000_000,
            transcendentals=0,
        ),
    )(
        in_hbm(source_lengths),
        in_hbm(expert_ids.transpose(0, 2, 1)),
        in_hbm(expert_gates.transpose(0, 2, 1)),
        in_hbm(cross_query),
        in_hbm(enc_states.reshape(rows, width)),
        in_hbm(norm_gain.reshape(1, width)),
        in_hbm(final_gain.reshape(1, width)),
        in_hbm(w_key),
        in_hbm(w_value),
        in_hbm(w_in[0]),
        in_hbm(w_out[0]),
    )
    return encoded.reshape(sent, length, width), context


def solution(mesh):
    return jax.shard_map(
        functools.partial(on_device, mesh.shape["dev"]),
        mesh=mesh,
        in_specs=(
            P("dev", None, None),
            P(),
            P(),
            P("dev", None, None),
            P("dev", None, None),
            P("dev"),
            P("dev", None, "grp"),
            P("dev", "grp", None),
            P("dev", "grp"),
            P("dev", "grp"),
            P("dev", "grp"),
        ),
        out_specs=(P("dev", None, None), P("dev", "grp")),
        check_vma=False,
    )
```

```python
import functools
import math

import jax
import jax.numpy as jnp
from jax import lax
from jax.experimental import pallas as pl
from jax.experimental.pallas import tpu as pltpu
from jax.sharding import PartitionSpec as P

HEADS = 16
HEAD_DIM = 128
CAPACITY = 8
AHEAD = 3
UNROLL = 6
ORDER = (
    ("a", 0), ("a", 1), ("k", 0), ("b", 0), ("a", 2), ("p", 0),
    ("b", 1), ("a", 3), ("c", 0), ("p", 1), ("b", 2), ("c", 1),
    ("p", 2), ("d", 0), ("k", 1), ("b", 3), ("c", 2), ("p", 3),
    ("d", 1), ("k", 2), ("e", 0), ("c", 3), ("d", 2), ("k", 3),
    ("e", 1), ("d", 3), ("e", 2), ("k", 4), ("e", 3),
)
EPSILON = 1e-05
F32 = jnp.float32
BF16 = jnp.bfloat16
MESH = pl.DeviceIdType.MESH


def layer_kernel(
    n_exp,
    n_x,
    lens_ref,
    ids_ref,
    gates_ref,
    query_ref,
    enc_hbm,
    ngain_hbm,
    fgain_hbm,
    wkey_hbm,
    wvalue_hbm,
    win_hbm,
    wout_hbm,
    out_ref,
    context_ref,
    enc_ref,
    ngain_ref,
    fgain_ref,
    wkv,
    win,
    wout,
    qkey,
    normed,
    dispatch,
    xbuf,
    combine,
    xrow,
    hid,
    hidden_sum,
    part,
    st1,
    rv1,
    st2,
    rv2,
    back,
    ybuf,
    mix,
    w_sem,
    a2a_send,
    a2a_recv,
    yag_send,
    yag_recv,
    rs_send,
    rs_recv,
    ret_send,
    ret_recv,
    mix_send,
    mix_recv,
    kvx_send,
    kvx_recv,
    kvz_send,
    kvz_recv,
    kvc_send,
    kvc_recv,
):
    rows, width = enc_ref.shape
    sent, _, length = ids_ref.shape
    quarter = width // 4
    half = quarter // 2
    per = n_exp // n_x
    crow = per * CAPACITY
    mrow = per * 2 * CAPACITY
    prow = normed.shape[0]

    g = lax.axis_index("grp")
    d = lax.axis_index("dev")
    my_x = d // per
    my_z = d % per
    right, left, diag = (g + 1) % 4, (g + 3) % 4, (g + 2) % 4

    loads = [
        pltpu.make_async_copy(src, dst, w_sem.at[i])
        for i, (src, dst) in enumerate(
            (
                (enc_hbm, enc_ref),
                (ngain_hbm, ngain_ref),
                (wkey_hbm, wkv.at[my_x, my_z, 0]),
                (wvalue_hbm, wkv.at[my_x, my_z, 1]),
                (win_hbm, win),
                (wout_hbm, wout),
                (fgain_hbm, fgain_ref),
            )
        )
    ]
    for load in loads:
        load.start()

    barrier = pltpu.get_barrier_semaphore()

    def greet(i, carry):
        pl.semaphore_signal(barrier, inc=1, device_id=(g, (d + i) % n_exp), device_id_type=MESH)
        return carry

    lax.fori_loop(1, n_exp, greet, 0)
    for i in range(1, 4):
        pl.semaphore_signal(barrier, inc=1, device_id=((g + i) % 4, d), device_id_type=MESH)

    def arrived(ref, sem):
        pltpu.make_async_copy(ref, ref, sem).wait()

    loads[0].wait()
    loads[1].wait()

    blk = 16
    qcols = pl.ds(pl.multiple_of(g * quarter, 128), quarter)

    def norm_block(i, carry):
        r = pl.ds(pl.multiple_of(i * blk, blk), blk)
        v = enc_ref[r, :].astype(F32)
        mean = jnp.mean(v, axis=-1, keepdims=True)
        c = v - mean
        var = jnp.mean(c * c, axis=-1, keepdims=True)
        own = enc_ref[r, qcols].astype(F32) - mean
        own = own * lax.rsqrt(var + EPSILON) * ngain_ref[:, qcols]
        normed[r, :] = own.astype(BF16)
        return carry

    lax.fori_loop(0, rows // blk, norm_block, 0)
    if prow > rows:
        normed[rows:, :] = jnp.zeros((prow - rows, quarter), BF16)

    def along(ref, k):
        return jnp.concatenate([ref[i, k : k + 1, :] for i in range(sent)], axis=1)

    pos = lax.broadcasted_iota(jnp.int32, (1, rows), 1)
    live = jnp.zeros((1, rows), jnp.bool_)
    for i in range(sent):
        live = live | ((pos >= i * length) & (pos < i * length + lens_ref[i]))
    expert = lax.broadcasted_iota(jnp.int32, (n_exp, rows), 0)
    earlier = (
        lax.broadcasted_iota(jnp.int32, (rows, rows), 0)
        < lax.broadcasted_iota(jnp.int32, (rows, rows), 1)
    ).astype(BF16)
    codes = []
    offset = jnp.zeros((n_exp, 1), F32)
    for k in range(2):
        hot = jnp.where((along(ids_ref, k) == expert) & live, 1.0, 0.0).astype(F32)
        rank = jnp.dot(hot.astype(BF16), earlier, preferred_element_type=F32) + offset
        offset = offset + jnp.sum(hot, axis=1, keepdims=True)
        code = jnp.sum(
            hot * (rank + (2 * CAPACITY) * expert.astype(F32)), axis=0, keepdims=True
        )
        codes.append(jnp.where(live, code, -100.0))
    line = lax.broadcasted_iota(jnp.int32, (128, rows), 0)
    facts = jnp.zeros((128, rows), F32)
    for i, fact in enumerate(codes + [along(gates_ref, 0), along(gates_ref, 1)]):
        facts = jnp.where(line == i, fact, facts)
    if prow > rows:
        facts = jnp.concatenate([facts, jnp.zeros((128, prow - rows), F32)], axis=1)
        codes = [
            jnp.concatenate([v, jnp.full((1, prow - rows), -100.0, F32)], axis=1) for v in codes
        ]
    row0, row1 = codes[0].astype(jnp.int32), codes[1].astype(jnp.int32)
    columns = facts.T
    code0 = columns[:rows, 0:1].astype(jnp.int32)
    code1 = columns[:rows, 1:2].astype(jnp.int32)
    gate0, gate1 = columns[:rows, 2:3], columns[:rows, 3:4]

    for c in range(n_x):
        base = ((my_x + c) % n_x) * mrow
        r = lax.broadcasted_iota(jnp.int32, (mrow, prow), 0) + base
        acc = jnp.zeros((mrow, half), F32)
        for h in range(2):
            rh = r - h * CAPACITY
            pick = jnp.where((rh == row0) | (rh == row1), 1.0, 0.0).astype(BF16)
            acc = acc + jnp.dot(
                pick, normed[:, h * half : (h + 1) * half], preferred_element_type=F32
            )
        dispatch[c] = acc.astype(BF16).reshape(per, 2 * CAPACITY, half)

    pl.semaphore_wait(barrier, n_exp - 1 + 3)

    def dispatch_chunk(c):
        def send(j, carry):
            z = (my_z + j) % per
            pltpu.make_async_remote_copy(
                src_ref=dispatch.at[c, z],
                dst_ref=xbuf.at[g, d],
                send_sem=a2a_send.at[c],
                recv_sem=a2a_recv.at[c],
                device_id=(g, ((my_x + c) % n_x) * per + z),
                device_id_type=MESH,
            ).start()
            return carry

        if c == 0:
            pltpu.make_async_copy(
                dispatch.at[0, my_z], xbuf.at[g, d], a2a_recv.at[0]
            ).start()
            lax.fori_loop(1, per, send, 0)
        else:
            lax.fori_loop(0, per, send, 0)

    for c in range(min(AHEAD, n_x)):
        dispatch_chunk(c)

    n_z = per // 2
    my_zz, my_core = my_z // 2, my_z % 2
    kv_sends = []

    def kv_copy(ref, send_sem, recv_sem, to_x, to_z):
        cp = pltpu.make_async_remote_copy(
            src_ref=ref,
            dst_ref=ref,
            send_sem=send_sem,
            recv_sem=recv_sem,
            device_id=(g, to_x * per + to_z),
            device_id_type=MESH,
        )
        cp.start()
        kv_sends.append(cp)

    loads[2].wait()
    loads[3].wait()
    for i in range(1, n_x):
        kv_copy(
            wkv.at[my_x, my_z],
            kvx_send.at[i],
            kvx_recv.at[i],
            (my_x + i) % n_x,
            my_z,
        )

    def kv_piece(way, step, core):
        shift = step if way == 1 else n_z - step
        z = 2 * ((my_zz + shift) % n_z) + core
        if step < n_z // 2 or step == 0:
            return wkv.at[:, z]
        return wkv.at[:, z, way]

    def kv_event(step):
        if step > n_z // 2:
            return
        other = 2 * my_zz + (1 - my_core)
        if step == 0:
            for i in range(1, n_x):
                arrived(wkv.at[(my_x + n_x - i) % n_x, my_z], kvx_recv.at[i])
            kv_copy(kv_piece(0, 0, my_core), kvc_send.at[0, 0], kvc_recv.at[0, 0], my_x, other)
        for way in range(2):
            if step > 0:
                arrived(kv_piece(way, step, my_core), kvz_recv.at[way, step])
            if step < n_z // 2:
                ref = kv_piece(way, step, my_core)
                if step + 1 == n_z // 2:
                    shift = step if way == 1 else n_z - step
                    ref = wkv.at[:, 2 * ((my_zz + shift) % n_z) + my_core, way]
                to = 2 * ((my_zz + (1 if way == 0 else n_z - 1)) % n_z) + my_core
                kv_copy(ref, kvz_send.at[way, step], kvz_recv.at[way, step + 1], my_x, to)
            if step > 0:
                kv_copy(
                    kv_piece(way, step, my_core),
                    kvc_send.at[way, step],
                    kvc_recv.at[way, step],
                    my_x,
                    other,
                )

    def kv_finish():
        arrived(kv_piece(0, 0, 1 - my_core), kvc_recv.at[0, 0])
        for step in range(1, n_z // 2 + 1):
            for way in range(2):
                arrived(kv_piece(way, step, 1 - my_core), kvc_recv.at[way, step])

    for c in range(n_x):
        base = ((my_x + c) % n_x) * mrow
        col = lax.broadcasted_iota(jnp.int32, (rows, mrow), 1) + base
        for h in range(2):
            ch = col - h * CAPACITY
            value = jnp.where(ch == code0, gate0, jnp.where(ch == code1, gate1, 0.0))
            high = value.astype(BF16)
            combine[c, 2 * h * rows : (2 * h + 1) * rows, :] = high
            combine[c, (2 * h + 1) * rows : (2 * h + 2) * rows, :] = (
                value - high.astype(F32)
            ).astype(BF16)

    def slab(c):
        return ((my_x + n_x - c) % n_x) * per

    def ycopy(src, dst, send_sem, recv_sem, to):
        return pltpu.make_async_remote_copy(
            src_ref=src,
            dst_ref=dst,
            send_sem=send_sem,
            recv_sem=recv_sem,
            device_id=(to, d),
            device_id_type=MESH,
        )

    def xs(q, c, start=0, size=per):
        return xbuf.at[q, pl.ds(slab(c) + start, size)]

    hp = per // 2
    sends = []

    def stage_a(c):
        arrived(xs(g, c), a2a_recv.at[c])
        if c + AHEAD < n_x:
            dispatch_chunk(c + AHEAD)
        for i, to in enumerate((right, left)):
            cp = ycopy(xs(g, c), xs(g, c), yag_send.at[c, i], yag_recv.at[c, i], to)
            cp.start()
            sends.append(cp)

    def stage_b(c):
        arrived(xs(left, c), yag_recv.at[c, 0])
        cp = ycopy(
            xs(left, c, 0, hp), xs(left, c, 0, hp), yag_send.at[c, 2], yag_recv.at[c, 2], right
        )
        cp.start()
        sends.append(cp)
        arrived(xs(right, c), yag_recv.at[c, 1])
        cp = ycopy(
            xs(right, c, hp, hp), xs(right, c, hp, hp), yag_send.at[c, 3], yag_recv.at[c, 3], left
        )
        cp.start()
        sends.append(cp)

    hrow = crow // 2

    tile = min(256, hid.shape[1])

    def place(k, q, c):
        block = xbuf[q, pl.ds(slab(c), per)].astype(F32)
        for h in range(2):
            xrow[:, k * quarter + h * half : k * quarter + (h + 1) * half] = (
                block[:, h * CAPACITY : (h + 1) * CAPACITY, :].reshape(crow, half).astype(BF16)
            )

    def term(k, q, cs):
        features = pl.ds(pl.multiple_of(q * quarter, 128), quarter)
        return jnp.dot(
            xrow[:, k * quarter : (k + 1) * quarter],
            win[features, cs],
            preferred_element_type=F32,
        )

    def stage_p(c):
        if c == 0:
            loads[4].wait()
        early = (g, left, right)
        for k, q in enumerate(early):
            place(k, q, c)

        def add_early(n, carry):
            cs = pl.ds(pl.multiple_of(n * tile, tile), tile)
            hidden_sum[c, :, cs] = term(0, g, cs) + term(1, left, cs) + term(2, right, cs)
            return carry

        lax.fori_loop(0, hid.shape[1] // tile, add_early, 0)

    def stage_c(c):
        arrived(xs(diag, c, 0, hp), yag_recv.at[c, 2])
        arrived(xs(diag, c, hp, hp), yag_recv.at[c, 3])
        place(3, diag, c)

        def add_last(n, carry):
            cs = pl.ds(pl.multiple_of(n * tile, tile), tile)
            total = hidden_sum[c, :, cs] + term(3, diag, cs)
            hid[:, cs] = jnp.maximum(total, 0.0).astype(BF16)
            return carry

        lax.fori_loop(0, hid.shape[1] // tile, add_last, 0)
        if c == 0:
            loads[5].wait()

        def second(q):
            cs = pl.ds(pl.multiple_of(q * quarter, 128), quarter)
            return jnp.dot(hid[...], wout[:, cs], preferred_element_type=F32)

        st1[c] = second(diag).astype(BF16)
        for i, to in enumerate((right, left)):
            cp = ycopy(
                st1.at[c, pl.ds(i * hrow, hrow)],
                rv1.at[c, pl.ds(i * hrow, hrow)],
                rs_send.at[c, i],
                rs_recv.at[c, i],
                to,
            )
            cp.start()
            sends.append(cp)

        part[c, 0] = second(right)
        part[c, 1] = second(left)
        part[c, 2] = second(g)

    def stage_d(c):
        for i, to in enumerate((right, left)):
            a, b = i * hrow, (1 - i) * hrow
            arrived(rv1.at[c, pl.ds(a, hrow)], rs_recv.at[c, i])
            st2[c, i, a : a + hrow, :] = (
                part[c, i, a : a + hrow, :] + rv1[c, a : a + hrow, :].astype(F32)
            ).astype(BF16)
            st2[c, i, b : b + hrow, :] = part[c, i, b : b + hrow, :].astype(BF16)
            cp = ycopy(st2.at[c, i], rv2.at[c, i], rs_send.at[c, 2 + i], rs_recv.at[c, 2 + i], to)
            cp.start()
            sends.append(cp)

    def stage_e(c):
        for i in range(2):
            arrived(rv2.at[c, i], rs_recv.at[c, 2 + i])
        total = part[c, 2] + rv2[c, 0].astype(F32) + rv2[c, 1].astype(F32)
        total = total.reshape(per, CAPACITY, quarter)
        back[c] = jnp.concatenate([total[:, :, :half], total[:, :, half:]], axis=1).astype(BF16)

        def send(j, carry):
            z = (my_z + j + (0 if c == 0 else per // 2)) % per
            pltpu.make_async_remote_copy(
                src_ref=back.at[c, z],
                dst_ref=ybuf.at[d],
                send_sem=ret_send.at[c],
                recv_sem=ret_recv.at[c],
                device_id=(g, slab(c) + z),
                device_id_type=MESH,
            ).start()
            return carry

        if c == 0:
            pltpu.make_async_copy(back.at[0, my_z], ybuf.at[d], ret_recv.at[0]).start()
            lax.fori_loop(1, per, send, 0)
        else:
            lax.fori_loop(0, per, send, 0)

    stages = dict(p=stage_p, a=stage_a, b=stage_b, c=stage_c, d=stage_d, e=stage_e, k=kv_event)
    for name, index in ORDER:
        if name == "k" or index < n_x:
            stages[name](index)

    kv_finish()
    columns_kv = wkv.shape[-1]
    heads = columns_kv // HEAD_DIM
    pairs = sent * heads
    row = lax.broadcasted_iota(jnp.int32, (pairs, columns_kv), 0)
    own_head = row % heads == lax.broadcasted_iota(jnp.int32, (pairs, columns_kv), 1) // HEAD_DIM
    query = jnp.zeros((pairs, columns_kv), F32)
    for i in range(sent):
        query = jnp.where(row // heads == i, query_ref[i : i + 1, :].astype(F32), query)
    query = jnp.where(own_head, query, 0.0).astype(BF16)

    def projection(kv):
        return wkv[:, :, kv].reshape(width, columns_kv)

    through = lax.dot_general(
        query, projection(0), (((1,), (1,)), ((), ())), preferred_element_type=F32
    )
    high = through.astype(BF16)
    qkey[:pairs, :] = high.astype(F32)
    qkey[pairs:, :] = through - high.astype(F32)

    acc = jnp.zeros((4 * rows, half), F32)
    for c in range(n_x):
        here = pl.ds(((my_x + c) % n_x) * per, per)
        arrived(ybuf.at[here], ret_recv.at[c])
        acc = acc + jnp.dot(
            combine[c], ybuf[here].reshape(mrow, half), preferred_element_type=F32
        )
    mix[g] = jnp.concatenate(
        [acc[:rows] + acc[rows : 2 * rows], acc[2 * rows : 3 * rows] + acc[3 * rows :]], axis=1
    ).astype(BF16)

    hm = rows // 2

    def mix_part(q, i):
        return mix.at[q, pl.ds(i * hm, hm)]

    for turn in range(2):
        for way, to in enumerate((right, left)):
            i = (way + turn) % 2
            cp = ycopy(
                mix_part(g, i), mix_part(g, i), mix_send.at[way, i], mix_recv.at[way, i], to
            )
            cp.start()
            sends.append(cp)
    for way, (origin, to) in enumerate(((left, right), (right, left))):
        arrived(mix_part(origin, way), mix_recv.at[way, way])
        cp = ycopy(
            mix_part(origin, way),
            mix_part(origin, way),
            mix_send.at[way, 2],
            mix_recv.at[way, 2],
            to,
        )
        cp.start()
        sends.append(cp)
    for way, origin in enumerate((left, right)):
        arrived(mix_part(origin, 1 - way), mix_recv.at[way, 1 - way])
    for way in range(2):
        arrived(mix_part(diag, way), mix_recv.at[way, 2])

    def final_block(i, carry):
        r = pl.ds(pl.multiple_of(i * blk, blk), blk)
        m = jnp.concatenate([mix[q, r, :] for q in range(4)], axis=1)
        v = enc_ref[r, :].astype(F32) + m.astype(F32)
        mean = jnp.mean(v, axis=-1, keepdims=True)
        cen = v - mean
        var = jnp.mean(cen * cen, axis=-1, keepdims=True)
        out_ref[r, :] = (cen * lax.rsqrt(var + EPSILON) * fgain_ref[...]).astype(BF16)
        return carry

    loads[6].wait()
    lax.fori_loop(0, rows // blk, final_block, 0, unroll=UNROLL)

    scores = lax.dot_general(
        qkey[...].astype(BF16), out_ref[...], (((1,), (1,)), ((), ())), preferred_element_type=F32
    )
    scores = (scores[:pairs] + scores[pairs:]) * (1.0 / math.sqrt(HEAD_DIM))
    which = lax.broadcasted_iota(jnp.int32, (pairs, rows), 0) // heads
    at = lax.broadcasted_iota(jnp.int32, (pairs, rows), 1)
    inside = jnp.zeros((pairs, rows), jnp.bool_)
    for i in range(sent):
        inside = inside | (
            (which == i) & (at >= i * length) & (at < i * length + lens_ref[i])
        )
    weights = jnp.where(inside, jnp.exp(scores), 0.0)
    probabilities = (weights / jnp.sum(weights, axis=-1, keepdims=True)).astype(BF16)
    mean_state = jnp.dot(probabilities, out_ref[...], preferred_element_type=F32)
    high = mean_state.astype(BF16)
    low = (mean_state - high.astype(F32)).astype(BF16)
    terms = jnp.dot(
        jnp.concatenate([high, low], axis=0), projection(1), preferred_element_type=F32
    )
    context = jnp.where(own_head, terms[:pairs] + terms[pairs:], 0.0)
    for i in range(sent):
        context_ref[i : i + 1, :] = jnp.sum(
            jnp.where(row // heads == i, context, 0.0), axis=0, keepdims=True
        ).astype(BF16)

    for cp in sends + kv_sends:
        cp.wait_send()
    for c in range(n_x):
        count = per - 1 if c == 0 else per
        for buf, sem in ((dispatch, a2a_send), (back, ret_send)):
            arrived(buf.at[c, pl.ds(0, count)], sem.at[c])


def in_hbm(array):
    return pltpu.with_memory_space_constraint(array, pltpu.HBM)


def on_device(
    n_exp,
    enc_states,
    norm_gain,
    final_gain,
    expert_ids,
    expert_gates,
    source_lengths,
    w_in,
    w_out,
    w_key,
    w_value,
    cross_query,
):
    sent, length, width = enc_states.shape
    rows = sent * length
    n_x = 1 if n_exp == 16 else min(4, n_exp // 2)
    per = n_exp // n_x
    n_z = per // 2
    quarter, half = width // 4, width // 8
    crow, mrow = per * CAPACITY, per * 2 * CAPACITY
    ff = w_in.shape[2]
    kv_rows, kv_columns = w_key.shape
    pairs = sent * (kv_columns // HEAD_DIM)
    prow = -(-rows // 128) * 128
    vmem = pl.BlockSpec(memory_space=pltpu.VMEM)
    hbm = pl.BlockSpec(memory_space=pltpu.HBM)
    smem = pl.BlockSpec(memory_space=pltpu.SMEM)
    dma = pltpu.SemaphoreType.DMA
    encoded, context = pl.pallas_call(
        functools.partial(layer_kernel, n_exp, n_x),
        out_shape=(
            jax.ShapeDtypeStruct((rows, width), BF16),
            jax.ShapeDtypeStruct(cross_query.shape, BF16),
        ),
        in_specs=[smem, vmem, vmem, vmem] + [hbm] * 7,
        out_specs=(vmem, vmem),
        scratch_shapes=[
            pltpu.VMEM((rows, width), BF16),
            pltpu.VMEM((1, width), F32),
            pltpu.VMEM((1, width), F32),
            pltpu.VMEM((n_x, per, 2, kv_rows, kv_columns), BF16),
            pltpu.VMEM(w_in.shape[1:], BF16),
            pltpu.VMEM(w_out.shape[1:], BF16),
            pltpu.VMEM((2 * pairs, width), F32),
            pltpu.VMEM((prow, quarter), BF16),
            pltpu.VMEM((n_x, per, 2 * CAPACITY, half), BF16),
            pltpu.VMEM((4, n_exp, 2 * CAPACITY, half), BF16),
            pltpu.VMEM((n_x, 4 * rows, mrow), BF16),
            pltpu.VMEM((crow, width), BF16),
            pltpu.VMEM((crow, ff), BF16),
            pltpu.VMEM((n_x, crow, ff), F32),
            pltpu.VMEM((n_x, 3, crow, quarter), F32),
            pltpu.VMEM((n_x, crow, quarter), BF16),
            pltpu.VMEM((n_x, crow, quarter), BF16),
            pltpu.VMEM((n_x, 2, crow, quarter), BF16),
            pltpu.VMEM((n_x, 2, crow, quarter), BF16),
            pltpu.VMEM((n_x, per, 2 * CAPACITY, half), BF16),
            pltpu.VMEM((n_exp, 2 * CAPACITY, half), BF16),
            pltpu.VMEM((4, rows, quarter), BF16),
            dma((7,)),
            dma((n_x,)),
            dma((n_x,)),
            dma((n_x, 4)),
            dma((n_x, 4)),
            dma((n_x, 4)),
            dma((n_x, 4)),
            dma((n_x,)),
            dma((n_x,)),
            dma((2, 3)),
            dma((2, 3)),
            dma((n_x,)),
            dma((n_x,)),
            dma((2, n_z // 2 + 1)),
            dma((2, n_z // 2 + 1)),
            dma((2, n_z // 2 + 1)),
            dma((2, n_z // 2 + 1)),
        ],
        compiler_params=pltpu.CompilerParams(
            collective_id=0, has_side_effects=True, vmem_limit_bytes=40 * 1024 * 1024
        ),
        cost_estimate=pl.CostEstimate(
            flops=4 * n_exp * CAPACITY * width * ff,
            bytes_accessed=12_000_000,
            transcendentals=0,
        ),
    )(
        in_hbm(source_lengths),
        in_hbm(expert_ids.transpose(0, 2, 1)),
        in_hbm(expert_gates.transpose(0, 2, 1)),
        in_hbm(cross_query),
        in_hbm(enc_states.reshape(rows, width)),
        in_hbm(norm_gain.reshape(1, width)),
        in_hbm(final_gain.reshape(1, width)),
        in_hbm(w_key),
        in_hbm(w_value),
        in_hbm(w_in[0]),
        in_hbm(w_out[0]),
    )
    return encoded.reshape(sent, length, width), context


def solution(mesh):
    return jax.shard_map(
        functools.partial(on_device, mesh.shape["dev"]),
        mesh=mesh,
        in_specs=(
            P("dev", None, None),
            P(),
            P(),
            P("dev", None, None),
            P("dev", None, None),
            P("dev"),
            P("dev", None, "grp"),
            P("dev", "grp", None),
            P("dev", "grp"),
            P("dev", "grp"),
            P("dev", "grp"),
        ),
        out_specs=(P("dev", None, None), P("dev", "grp")),
        check_vma=False,
    )
```
